128 devices in a mesh: node: 16 (over y, z), cls: 8 (over x, core).
Axes of the slice: x: 4, y: 4, z: 4, core: 2. Of those that a mesh axis runs over, the one named last changes fastest.
Arguments:
- seed_scores: float32 [24576, 1024], P('node', 'cls'), may hold values from -6 to 6
- tile_vals: bfloat16 [192, 17, 128, 128], P('node'), may hold values from 0 to 1, as said below
- tile_cols: int32 [192, 17], P('node'), may hold values from 0 to 191, as said below
- tile_count: int32 [192], P('node'), may hold values from 1 to 17, as said below
- tile_scale: float32 [192, 17], P('node'), as said below
Outputs:
- solution: float32 [24576, 1024], P('node', 'cls')
- residual: float32 [24576, 1024], P('node', 'cls')
The draws below stay inside these ranges and needn't reach their ends.
Inputs may be any that keep to these rules, and one draw needn't show every extreme that they name: `tile_cols`: slot s of block i names block (i + o) mod 192 for an offset o with |o| <= 8, each offset once in a block row; the first tile_count[i] slots hold the tiles present, the diagonal block first. Block i holds a tile of block j exactly when block j holds one of block i, and the two tiles are transposes with equal scales. `tile_count`: some block row holds all 17 tiles. `tile_vals`: tiles on the diagonal block are symmetric. Slots past tile_count hold arbitrary entries. `tile_scale`: every scale lies between 1.2 / (min(128, 16) * 17) and 1.8 / min(128, 16).
All inputs are finite; a program needn't handle non-finite values.
Results may differ from the reference program's by a relative error of at most 0.0065.
The reference program's roundings to bfloat16 on the way count: a program that leaves them out, or rounds other values in their place, can miss the bound.
Values may be sent and summed in bfloat16 or wider, within the bound.
A program may use at most 320 MiB of HBM per device.

```python
import jax
import jax.numpy as jnp
from jax import lax

TILE = 128
REACH = 8
NB_DEV = 12
SLOTS = 17
BLOCKS = 192
NODES = 24576
CLASSES = 1024


def tile_pattern(key):
    key = jax.random.fold_in(key, 11)
    level_key, roll_key = jax.random.split(key)
    owners = jnp.arange(BLOCKS) // NB_DEV
    levels = jax.random.randint(level_key, (BLOCKS // NB_DEV,), 0, 8)
    rolled = jax.random.randint(roll_key, (BLOCKS, REACH), 0, 49)
    threshold = (levels * levels)[owners]
    forward = rolled < threshold[:, None]
    block_ids = jnp.arange(BLOCKS)[:, None]
    offsets = jnp.arange(1, REACH + 1)[None, :]
    forced = (block_ids == 0) | (jnp.mod(block_ids + offsets, BLOCKS) == 0)
    forward = forward | forced
    backward = forward[jnp.mod(block_ids - offsets, BLOCKS), offsets - 1]
    live_slot = jnp.concatenate([jnp.ones((BLOCKS, 1), jnp.int32), forward.astype(jnp.int32), backward.astype(jnp.int32)], axis=1)
    slot_order = jnp.argsort(1 - live_slot, axis=1, stable=True)
    return (live_slot, slot_order)


def mirror_index():
    block_ids = jnp.arange(BLOCKS)[:, None]
    offsets = jnp.arange(1, REACH + 1)[None, :]
    return (jnp.mod(block_ids - offsets, BLOCKS), offsets - 1)


def nonzero_share():
    return min(1.0, 16.0 / TILE)


def draw_tile_cols(key, part):
    live_slot, slot_order = tile_pattern(key)
    shifts = jnp.concatenate([jnp.zeros((1,), jnp.int32), jnp.arange(1, REACH + 1), -jnp.arange(1, REACH + 1)]).astype(jnp.int32)
    columns = jnp.mod(jnp.arange(BLOCKS)[:, None] + shifts[None, :], BLOCKS)
    return jnp.take_along_axis(columns, slot_order, axis=1).astype(jnp.int32)


def draw_tile_count(key, part):
    live_slot, slot_order = tile_pattern(key)
    return jnp.sum(live_slot, axis=1).astype(jnp.int32)


def draw_tile_vals(key, part):
    live_slot, slot_order = tile_pattern(key)
    key = jax.random.fold_in(key, 5)
    own_key, pair_key, spare_key, own_mask_key, pair_mask_key = jax.random.split(key, 5)
    share = nonzero_share()
    paired = jax.random.uniform(pair_key, (BLOCKS, REACH, TILE, TILE), jnp.float32)
    paired = jnp.where(jax.random.bernoulli(pair_mask_key, share, paired.shape), paired, 0.0)
    own_raw = jax.random.uniform(own_key, (BLOCKS, TILE, TILE), jnp.float32)
    own_raw = jnp.where(jax.random.bernoulli(own_mask_key, share, own_raw.shape), own_raw, 0.0)
    own_tile = 0.5 * (own_raw + jnp.swapaxes(own_raw, 1, 2))
    spare = jax.random.uniform(spare_key, (BLOCKS, SLOTS, TILE, TILE), jnp.float32)
    source_rows, source_cols = mirror_index()
    mirrored = jnp.swapaxes(paired[source_rows, source_cols], 2, 3)
    slotted = jnp.concatenate([own_tile[:, None], paired, mirrored], axis=1)
    slotted = jnp.where(live_slot[:, :, None, None] > 0, slotted, spare)
    return jnp.take_along_axis(slotted, slot_order[:, :, None, None], axis=1).astype(jnp.bfloat16)


def log_between(key, shape, lowest, highest):
    return jnp.exp(jax.random.uniform(key, shape, jnp.float32, jnp.log(lowest), jnp.log(highest)))


def draw_tile_scale(key, part):
    live_slot, slot_order = tile_pattern(key)
    key = jax.random.fold_in(key, 7)
    own_key, pair_key, spare_key = jax.random.split(key, 3)
    row_total = TILE * nonzero_share() / 2.0
    counts = jnp.sum(live_slot, axis=1).astype(jnp.float32)
    partner = jnp.mod(jnp.arange(BLOCKS)[:, None] + jnp.arange(1, REACH + 1)[None, :], BLOCKS)
    paired = log_between(pair_key, (BLOCKS, REACH), 0.6, 0.9) / (row_total * jnp.sqrt(counts[:, None] * counts[partner]))
    own_scale = log_between(own_key, (BLOCKS, 1), 0.6, 0.9) / (row_total * counts[:, None])
    spare = log_between(spare_key, (BLOCKS, SLOTS), 0.6 / (row_total * SLOTS), 0.9 / row_total)
    source_rows, source_cols = mirror_index()
    mirrored = paired[source_rows, source_cols]
    slotted = jnp.concatenate([own_scale, paired, mirrored], axis=1)
    slotted = jnp.where(live_slot > 0, slotted, spare)
    return jnp.take_along_axis(slotted, slot_order, axis=1).astype(jnp.float32)


def draw_seed_scores(key, part):
    key = jax.random.fold_in(key, 23)
    keys = jax.random.split(key, 9)
    freq_key, phase_key, amp_key, rough_key = (keys[0], keys[1], keys[2], keys[3])
    shared_key, share_key, factor_key, loading_key = (keys[5], keys[6], keys[7], keys[8])
    factor_count = max(2, min(64, CLASSES // 4))
    strengths = 0.4 * jnp.exp(jnp.linspace(0.0, jnp.log(0.01), factor_count)).astype(jnp.float32)
    loadings = jax.random.normal(loading_key, (factor_count, CLASSES), jnp.float32) * strengths[:, None]
    class_share = jax.random.uniform(share_key, (CLASSES,), jnp.float32, 0.7, 1.3)
    freq = jax.random.randint(freq_key, (CLASSES,), 1, 5).astype(jnp.float32)
    phase = jax.random.uniform(phase_key, (CLASSES,), jnp.float32, 0.0, 2.0 * jnp.pi)
    amp = jax.random.uniform(amp_key, (CLASSES,), jnp.float32, 0.3, 0.9)
    place = (jnp.arange(NODES).astype(jnp.float32) / NODES)[:, None]
    wave = jnp.cos(2.0 * jnp.pi * freq[None, :] * place + phase[None, :])
    factors = jnp.clip(jax.random.normal(factor_key, (NODES, factor_count), jnp.float32), -5.0, 5.0)
    shared = 0.8 * jnp.clip(jax.random.normal(shared_key, (NODES,), jnp.float32), -5.0, 5.0)
    rough = 0.2 * jnp.clip(jax.random.normal(rough_key, (NODES, CLASSES), jnp.float32), -5.0, 5.0)
    smooth = amp[None, :] * wave
    common = jnp.dot(factors, loadings, precision=lax.Precision.HIGHEST)
    total = smooth + rough + shared[:, None] * class_share[None, :] + common
    return jnp.clip(total, -6.0, 6.0).astype(jnp.float32)


def setup_inputs(seed: int = 0) -> dict:
    key_of = jax.random.split(jax.random.key(seed), 6)
    return {
        "seed_scores": draw_seed_scores(jax.random.fold_in(key_of[5], 71), 0),
        "tile_vals": draw_tile_vals(jax.random.fold_in(key_of[5], 71), 0),
        "tile_cols": draw_tile_cols(jax.random.fold_in(key_of[5], 71), 0),
        "tile_count": draw_tile_count(jax.random.fold_in(key_of[5], 71), 0),
        "tile_scale": draw_tile_scale(jax.random.fold_in(key_of[5], 71), 0),
    }


SHRINK = 0.9
PRECISE = lax.Precision.HIGHEST

def apply_operator(vector, tile_vals, tile_cols, tile_count, tile_scale):
    blocks_total = tile_vals.shape[0]
    slot_total = tile_vals.shape[1]
    tile_size = tile_vals.shape[2]
    packed = vector.astype(jnp.bfloat16).reshape(blocks_total, tile_size, vector.shape[1])
    live_mask = jnp.arange(slot_total)[None, :] < tile_count[:, None]
    weights = jnp.where(live_mask, tile_scale, jnp.zeros_like(tile_scale))
    summed = jnp.zeros(packed.shape, jnp.float32)
    for slot_index in range(slot_total):
        picked = jnp.take(packed, tile_cols[:, slot_index].astype(jnp.int32), axis=0).astype(jnp.float32)
        product = jnp.einsum('bij,bjc->bic', tile_vals[:, slot_index].astype(jnp.float32), picked, precision=PRECISE)
        summed = summed + weights[:, slot_index, None, None] * product
    return vector - SHRINK * summed.reshape(vector.shape)

def precondition(target, operate):
    estimate = target
    update = target
    factor = SHRINK
    for sweep_index in range(2):
        misfit = target - operate(estimate)
        factor_next = 1.0 / (2.0 / SHRINK - factor)
        update = factor_next * factor * update + 2.0 * factor_next / SHRINK * misfit
        estimate = estimate + update
        factor = factor_next
    return estimate

def reference(seed_scores, tile_vals, tile_cols, tile_count, tile_scale):

    def operate(vector):
        return apply_operator(vector, tile_vals, tile_cols, tile_count, tile_scale)
    direction = precondition(seed_scores, operate)
    imaged = operate(direction)
    curvature = jnp.dot(direction.T, imaged, precision=PRECISE)
    crossed = jnp.dot(direction.T, seed_scores, precision=PRECISE)
    lower_factor = jnp.linalg.cholesky(curvature)
    coefficients = jax.scipy.linalg.cho_solve((lower_factor, True), crossed)
    solution = jnp.dot(direction, coefficients, precision=PRECISE)
    residual = seed_scores - jnp.dot(imaged, coefficients, precision=PRECISE)
    return (solution, residual)
```

```python
import functools
import jax
import jax.numpy as jnp
from jax import lax
from jax.experimental import pallas as pl
from jax.experimental.pallas import tpu as pltpu
from jax.sharding import PartitionSpec as P

SHRINK = 0.9
HI = lax.Precision.HIGHEST
MESH = pl.DeviceIdType.MESH
T = 128


def remote(src, dst, send, recv, to):
    return pltpu.make_async_remote_copy(
        src_ref=src, dst_ref=dst, send_sem=send, recv_sem=recv, device_id=to, device_id_type=MESH)


def greet(peers):
    barrier = pltpu.get_barrier_semaphore()
    for peer in peers:
        pl.semaphore_signal(barrier, inc=1, device_id=peer, device_id_type=MESH)
    pl.semaphore_wait(barrier, len(peers))


def direction_kernel(slot_ref, weight_ref, seed_ref, tiles_ref,
                     d_ref, r_ref, image_ref, high_ref, ct_ref, xt_ref,
                     ext_ref, acc_ref, z_ref, low_ref, flat_ref,
                     halo_send, halo_recv, ring_send, ring_recv, pair_send, pair_recv):
    blocks = acc_ref.shape[0] // T
    reach = 8
    rows = blocks * T
    half = rows // 2
    edge = reach * T
    node, cls = lax.axis_index("node"), lax.axis_index("cls")
    nodes = lax.axis_size("node")
    chips = lax.axis_size("cls") // 2
    chip, core = cls // 2, cls % 2
    right_node, left_node = {"node": (node + 1) % nodes}, {"node": (node + nodes - 1) % nodes}
    right_chip, left_chip, far_chip = (chip + 1) % chips, (chip + chips - 1) % chips, (chip + 2) % chips
    right, left, twin = {"cls": right_chip * 2 + core}, {"cls": left_chip * 2 + core}, {"cls": chip * 2 + 1 - core}
    greet([right_node, left_node, right, left, twin])

    def halo_copies(s):
        ext = ext_ref.at[s]
        return (
            remote(ext.at[pl.ds(rows, edge)], ext.at[pl.ds(0, edge)],
                   halo_send.at[s, 0], halo_recv.at[s, 0], right_node),
            remote(ext.at[pl.ds(edge, edge)], ext.at[pl.ds(edge + rows, edge)],
                   halo_send.at[s, 1], halo_recv.at[s, 1], left_node),
        )

    def product(s, tile, source):
        return jnp.dot(tiles_ref[tile], ext_ref[s, pl.ds(pl.multiple_of(source * T, T), T), :],
                       preferred_element_type=jnp.float32)

    def spread(s, z):
        ext_ref[s, edge:edge + rows, :] = z.astype(jnp.bfloat16)
        copies = halo_copies(s)
        for copy in copies:
            copy.start()
        return copies

    def local_part(s):
        def one(i, _):
            total = jnp.zeros((T, T), jnp.float32)
            for j in range(blocks):
                o = j + reach - i
                fits = (o >= 0) & (o <= 2 * reach)
                at = i * (2 * reach + 1) + jnp.clip(o, 0, 2 * reach)
                w = jnp.where(fits, weight_ref[at], 0.0)
                total += w * product(s, slot_ref[at], j + reach)
            acc_ref[pl.ds(pl.multiple_of(i * T, T), T), :] = total
            return 0
        lax.fori_loop(0, blocks, one, 0)

    def edge_part(s):
        def one(t, _):
            low = jnp.zeros((T, T), jnp.float32)
            high = jnp.zeros((T, T), jnp.float32)
            for m in range(reach + 1):
                lower = m < reach - t
                i = jnp.where(lower, t, t + blocks - reach)
                j = t + m + jnp.where(lower, 0, blocks)
                at = i * (2 * reach + 1) + j - i
                w = weight_ref[at]
                p = product(s, slot_ref[at], j)
                low += jnp.where(lower, w, 0.0) * p
                high += jnp.where(lower, 0.0, w) * p
            acc_ref[pl.ds(pl.multiple_of(t * T, T), T), :] += low
            acc_ref[pl.ds(pl.multiple_of((t + blocks - reach) * T, T), T), :] += high
            return 0
        lax.fori_loop(0, reach, one, 0)

    def operate(s, copies):
        local_part(s)
        for copy in copies:
            copy.wait_recv()
        edge_part(s)

    factor = SHRINK
    z_ref[...] = seed_ref[...]
    d_ref[...] = seed_ref[...]
    for s in range(2):
        copies = spread(s, z_ref[...])
        operate(s, copies)
        factor_next = 1.0 / (2.0 / SHRINK - factor)
        misfit = seed_ref[...] - (z_ref[...] - SHRINK * acc_ref[...])
        update = factor_next * factor * d_ref[...] + (2.0 * factor_next / SHRINK) * misfit
        d_ref[...] = update
        z_ref[...] = z_ref[...] + update
        factor = factor_next
        for copy in copies:
            copy.wait_send()
    z = z_ref[...]
    d_ref[...] = z
    high = z.astype(jnp.bfloat16)
    high_ref[cls] = high
    low_ref[cls] = (z - high.astype(jnp.float32)).astype(jnp.bfloat16)
    copies = spread(2, z)

    def ring_copy(q, n, owner, part, to):
        ref = (high_ref, low_ref)[q].at[owner, pl.ds(part * half, half)]
        return remote(ref, ref, ring_send.at[q, n], ring_recv.at[q, n], to)

    def twin_copy(q, n, owner):
        ref = (high_ref, low_ref)[q].at[owner]
        return remote(ref, ref, pair_send.at[q, n], pair_recv.at[q, n], twin)

    first = []
    for q in range(2):
        first.append((ring_copy(q, 0, cls, 0, right), ring_copy(q, 1, cls, 1, left),
                      ring_copy(q, 2, cls, 1, right), ring_copy(q, 3, cls, 0, left)))
        for copy in first[q]:
            copy.start()
    own = [twin_copy(q, 0, cls) for q in range(2)]
    for copy in own:
        copy.start()
    operate(2, copies)
    image_ref[...] = z_ref[...] - SHRINK * acc_ref[...]
    r_ref[...] = seed_ref[...] - image_ref[...]

    image_t = image_ref[...].T
    r_t = r_ref[...].T
    for n, value in enumerate((image_t, r_t)):
        top = value.astype(jnp.bfloat16)
        flat_ref[n * T:(n + 1) * T, :] = top
        flat_ref[(2 + n) * T:(3 + n) * T, :] = (value - top.astype(jnp.float32)).astype(jnp.bfloat16)

    second = []
    for q in range(2):
        first[q][0].wait_recv()
        a = ring_copy(q, 4, left_chip * 2 + core, 0, right)
        a.start()
        first[q][1].wait_recv()
        b = ring_copy(q, 5, right_chip * 2 + core, 1, left)
        b.start()
        second.append((a, b))
        first[q][2].wait_recv()
        c = twin_copy(q, 1, left_chip * 2 + core)
        c.start()
        first[q][3].wait_recv()
        d = twin_copy(q, 2, right_chip * 2 + core)
        d.start()
        own.extend((c, d))

    def grams(q, which):
        g = (high_ref, low_ref)[q]
        both = jnp.concatenate([g[which * 2], g[which * 2 + 1]], axis=1)
        at = pl.ds(pl.multiple_of(which * 2 * T, 2 * T), 2 * T)
        if q == 0:
            out = jnp.dot(flat_ref[...], both, preferred_element_type=jnp.float32)
            ct_ref[:, at] = out[0:T] + out[2 * T:3 * T]
            xt_ref[:, at] = out[T:2 * T] + out[3 * T:]
        else:
            out = jnp.dot(flat_ref[0:2 * T, :], both, preferred_element_type=jnp.float32)
            ct_ref[:, at] += out[0:T]
            xt_ref[:, at] += out[T:]

    for q in range(2):
        own[q].wait_recv()
        grams(q, chip)
    far = []
    for q in range(2):
        for copy in second[q]:
            copy.wait_recv()
        e = twin_copy(q, 3, far_chip * 2 + core)
        e.start()
        far.append(e)
        own[2 + 2 * q].wait_recv()
        grams(q, left_chip)
        own[3 + 2 * q].wait_recv()
        grams(q, right_chip)
    for q in range(2):
        far[q].wait_recv()
        grams(q, far_chip)
    for copy in list(copies) + list(first[0]) + list(first[1]) + list(second[0]) + list(second[1]) + own + far:
        copy.wait_send()


def find_direction(slots, weights, seed, tiles):
    rows, width = seed.shape
    every = lax.axis_size("cls")
    f32 = jnp.float32
    vmem = pl.BlockSpec(memory_space=pltpu.VMEM)
    smem = pl.BlockSpec(memory_space=pltpu.SMEM)
    sems = pltpu.SemaphoreType.DMA
    return pl.pallas_call(
        direction_kernel,
        out_shape=[
            jax.ShapeDtypeStruct((rows, width), f32),
            jax.ShapeDtypeStruct((rows, width), f32),
            jax.ShapeDtypeStruct((rows, width), f32),
            jax.ShapeDtypeStruct((every, rows, width), jnp.bfloat16),
            jax.ShapeDtypeStruct((width, every * width), f32),
            jax.ShapeDtypeStruct((width, every * width), f32),
        ],
        in_specs=[smem, smem, vmem, vmem],
        out_specs=[vmem] * 6,
        scratch_shapes=[
            pltpu.VMEM((3, rows + 16 * T, width), jnp.bfloat16),
            pltpu.VMEM((rows, width), f32),
            pltpu.VMEM((rows, width), f32),
            pltpu.VMEM((every, rows, width), jnp.bfloat16),
            pltpu.VMEM((4 * T, rows), jnp.bfloat16),
            sems((3, 2)), sems((3, 2)), sems((2, 6)), sems((2, 6)), sems((2, 4)), sems((2, 4)),
        ],
        compiler_params=pltpu.CompilerParams(collective_id=0, has_side_effects=True, vmem_limit_bytes=48 << 20),
    )(slots, weights, seed, tiles)


def by_offset(tile_cols, tile_count, tile_scale):
    local_blocks, slot_total = tile_cols.shape
    reach = (slot_total - 1) // 2
    total = local_blocks * lax.axis_size("node")
    row = jnp.arange(local_blocks)[:, None]
    where = jnp.mod(tile_cols - (lax.axis_index("node") * local_blocks + row) + reach, total)
    slot = jnp.arange(slot_total)[None, :]
    weights = jnp.where(slot < tile_count[:, None], tile_scale, 0.0)
    hit = where[:, :, None] == jnp.arange(slot_total)[None, None, :]
    slots = jnp.sum(jnp.where(hit, (row * slot_total + slot)[:, :, None], 0), axis=1)
    return slots.reshape(-1), jnp.sum(jnp.where(hit, weights[:, :, None], 0.0), axis=1).reshape(-1)


def dot(a, b, dims=((1,), (0,))):
    return lax.dot_general(a, b, (dims, ((), ())), precision=HI, preferred_element_type=jnp.float32)

def row_of(x, j):
    return jnp.broadcast_to(x[j:j + 1, :], (8, T))

def factor(rows):
    lane = lax.broadcasted_iota(jnp.int32, (8, T), 1)
    sub = lax.broadcasted_iota(jnp.int32, (8, T), 0)
    out = []
    for k in range(16):
        cols = [[jnp.broadcast_to(r[:, 8 * k + j:8 * k + j + 1], (8, T)) for j in range(8)] for r in rows[k:]]
        inside = (lane >= 8 * k) & (lane < 8 * k + 8)
        unit = jnp.where(lane - 8 * k == sub, 1.0, 0.0)
        panel = jnp.where(inside, unit, rows[k])
        b = list(cols[0])
        done = jnp.zeros((8, T), jnp.float32)
        for j in range(8):
            p = row_of(b[j], j)
            r = 1.0 / p
            f = b[j]
            own = sub == j
            top = row_of(panel, j)
            done = jnp.where(own, top * lax.rsqrt(p), done)
            n = top * r
            panel = jnp.where(own, n, panel - f * n)
            for l in range(j + 1, 8):
                n = row_of(b[l], j) * r
                b[l] = jnp.where(own, n, b[l] - f * n)
        out.append(jnp.where(lane < 8 * k + 8, done, 0.0))
        spread = [row_of(panel, j) for j in range(8)]
        for g in range(k + 1, 16):
            acc = jnp.where(inside, 0.0, rows[g])
            for j in range(8):
                acc = acc - cols[g - k][j] * spread[j]
            rows[g] = acc
    return out

def solve_kernel(c_ref, x_ref, z_ref, a_ref, l_ref, v_ref):
    n = c_ref.shape[0]
    nb = n // T
    for i in range(nb):
        for j in range(i, nb):
            a_ref[i * T:(i + 1) * T, j * T:(j + 1) * T] = 0.5 * (
                c_ref[i * T:(i + 1) * T, j * T:(j + 1) * T] + c_ref[j * T:(j + 1) * T, i * T:(i + 1) * T].T)
    a_ref[:, n:] = x_ref[...]

    def step(k, _):
        base = pl.multiple_of(k * T, T)
        here = pl.ds(base, T)
        rows = [a_ref[pl.ds(base + 8 * g, 8), here] for g in range(16)]
        rows = factor(rows)
        for g in range(16):
            l_ref[pl.ds(base + 8 * g, 8), :] = rows[g]
        v_ref[here, :] = dot(l_ref[here, :], a_ref[here, :])
        def trail(i, _):
            at = pl.multiple_of(i * T, T)
            a_ref[pl.ds(at, T), :] -= dot(v_ref[here, pl.ds(at, T)], v_ref[here, :], ((0,), (0,)))
            return 0
        lax.fori_loop(k + 1, nb, trail, 0)
        return 0
    lax.fori_loop(0, nb, step, 0)
    def back(s, _):
        j = nb - 1 - s
        at = pl.multiple_of(j * T, T)
        known = dot(l_ref[pl.ds(at, T), :], v_ref[pl.ds(at, T), n:], ((0,), (0,)))
        z_ref[pl.ds(at, T), :] = known
        def one(i, _):
            to = pl.multiple_of(i * T, T)
            v_ref[pl.ds(to, T), n:] -= dot(v_ref[pl.ds(to, T), pl.ds(at, T)], known)
            return 0
        lax.fori_loop(0, j, one, 0)
        return 0
    lax.fori_loop(0, nb, back, 0)

def solve(c, x):
    n = c.shape[0]
    return pl.pallas_call(
        solve_kernel,
        out_shape=jax.ShapeDtypeStruct(x.shape, jnp.float32),
        in_specs=[pl.BlockSpec(memory_space=pltpu.VMEM)] * 2,
        out_specs=pl.BlockSpec(memory_space=pltpu.VMEM),
        scratch_shapes=[pltpu.VMEM((n, n + T), jnp.float32), pltpu.VMEM((n, T), jnp.float32),
                        pltpu.VMEM((n, n + T), jnp.float32)],
        compiler_params=pltpu.CompilerParams(vmem_limit_bytes=40 << 20),
    )(c, x)


def body(seed_scores, tile_vals, tile_cols, tile_count, tile_scale):
    slots, weights = by_offset(tile_cols, tile_count, tile_scale)
    tiles = tile_vals.reshape(-1, T, T)
    direction, misfit, imaged, high, ct, xt = find_direction(slots, weights, seed_scores, tiles)
    all_imaged = lax.all_gather(imaged, "cls", axis=1, tiled=True)
    ct, xt = lax.psum((ct, xt), "node")
    full = lax.all_gather(ct, "cls", axis=0, tiled=True)
    start = lax.axis_index("cls") * T
    mine = lax.dynamic_slice_in_dim(full, start, T, 1)
    rhs = (xt + 0.5 * (ct - mine.T)).T
    change = solve(full, rhs)
    packed = change.astype(jnp.bfloat16)
    mixed = sum(jnp.dot(high[n], packed[n * T:(n + 1) * T], preferred_element_type=jnp.float32) for n in range(high.shape[0]))
    solution = direction + mixed
    residual = misfit - jnp.dot(all_imaged, change, precision=HI)
    return (solution, residual)


def solution(mesh):
    return jax.shard_map(
        body,
        mesh=mesh,
        in_specs=(
            P("node", "cls"),
            P("node", None, None, None),
            P("node", None),
            P("node"),
            P("node", None),
        ),
        out_specs=(P("node", "cls"), P("node", "cls")),
        check_vma=False,
    )
```

```python
import functools
import jax
import jax.numpy as jnp
from jax import lax
from jax.experimental import pallas as pl
from jax.experimental.pallas import tpu as pltpu
from jax.sharding import PartitionSpec as P

SHRINK = 0.9
HI = lax.Precision.HIGHEST
MESH = pl.DeviceIdType.MESH
T = 128


def remote(src, dst, send, recv, to):
    return pltpu.make_async_remote_copy(
        src_ref=src, dst_ref=dst, send_sem=send, recv_sem=recv, device_id=to, device_id_type=MESH)


def greet(peers):
    barrier = pltpu.get_barrier_semaphore()
    for peer in peers:
        pl.semaphore_signal(barrier, inc=1, device_id=peer, device_id_type=MESH)
    pl.semaphore_wait(barrier, len(peers))


def direction_kernel(slot_ref, weight_ref, seed_ref, tiles_ref,
                     d_ref, r_ref, image_ref, high_ref, ct_ref, xt_ref,
                     ext_ref, acc_ref, z_ref, low_ref, flat_ref,
                     halo_send, halo_recv, ring_send, ring_recv, pair_send, pair_recv):
    blocks = acc_ref.shape[0] // T
    reach = 8
    rows = blocks * T
    half = rows // 2
    edge = reach * T
    node, cls = lax.axis_index("node"), lax.axis_index("cls")
    nodes = lax.axis_size("node")
    chips = lax.axis_size("cls") // 2
    chip, core = cls // 2, cls % 2
    right_node, left_node = {"node": (node + 1) % nodes}, {"node": (node + nodes - 1) % nodes}
    right_chip, left_chip, far_chip = (chip + 1) % chips, (chip + chips - 1) % chips, (chip + 2) % chips
    right, left, twin = {"cls": right_chip * 2 + core}, {"cls": left_chip * 2 + core}, {"cls": chip * 2 + 1 - core}
    greet([right_node, left_node, right, left, twin])

    def halo_copies(s):
        ext = ext_ref.at[s]
        return (
            remote(ext.at[pl.ds(rows, edge)], ext.at[pl.ds(0, edge)],
                   halo_send.at[s, 0], halo_recv.at[s, 0], right_node),
            remote(ext.at[pl.ds(edge, edge)], ext.at[pl.ds(edge + rows, edge)],
                   halo_send.at[s, 1], halo_recv.at[s, 1], left_node),
        )

    def product(s, tile, source):
        return jnp.dot(tiles_ref[tile], ext_ref[s, pl.ds(pl.multiple_of(source * T, T), T), :],
                       preferred_element_type=jnp.float32)

    def spread(s, z):
        ext_ref[s, edge:edge + rows, :] = z.astype(jnp.bfloat16)
        copies = halo_copies(s)
        for copy in copies:
            copy.start()
        return copies

    def local_part(s):
        def one(i, _):
            total = jnp.zeros((T, T), jnp.float32)
            for j in range(blocks):
                o = j + reach - i
                fits = (o >= 0) & (o <= 2 * reach)
                at = i * (2 * reach + 1) + jnp.clip(o, 0, 2 * reach)
                w = jnp.where(fits, weight_ref[at], 0.0)
                total += w * product(s, slot_ref[at], j + reach)
            acc_ref[pl.ds(pl.multiple_of(i * T, T), T), :] = total
            return 0
        lax.fori_loop(0, blocks, one, 0)

    def edge_part(s):
        def one(t, _):
            low = jnp.zeros((T, T), jnp.float32)
            high = jnp.zeros((T, T), jnp.float32)
            for m in range(reach + 1):
                lower = m < reach - t
                i = jnp.where(lower, t, t + blocks - reach)
                j = t + m + jnp.where(lower, 0, blocks)
                at = i * (2 * reach + 1) + j - i
                w = weight_ref[at]
                p = product(s, slot_ref[at], j)
                low += jnp.where(lower, w, 0.0) * p
                high += jnp.where(lower, 0.0, w) * p
            acc_ref[pl.ds(pl.multiple_of(t * T, T), T), :] += low
            acc_ref[pl.ds(pl.multiple_of((t + blocks - reach) * T, T), T), :] += high
            return 0
        lax.fori_loop(0, reach, one, 0)

    def operate(s, copies):
        local_part(s)
        for copy in copies:
            copy.wait_recv()
        edge_part(s)

    factor = SHRINK
    z_ref[...] = seed_ref[...]
    d_ref[...] = seed_ref[...]
    for s in range(2):
        copies = spread(s, z_ref[...])
        operate(s, copies)
        factor_next = 1.0 / (2.0 / SHRINK - factor)
        misfit = seed_ref[...] - (z_ref[...] - SHRINK * acc_ref[...])
        update = factor_next * factor * d_ref[...] + (2.0 * factor_next / SHRINK) * misfit
        d_ref[...] = update
        z_ref[...] = z_ref[...] + update
        factor = factor_next
        for copy in copies:
            copy.wait_send()
    z = z_ref[...]
    d_ref[...] = z
    high = z.astype(jnp.bfloat16)
    high_ref[cls] = high
    low_ref[cls] = (z - high.astype(jnp.float32)).astype(jnp.bfloat16)
    copies = spread(2, z)

    def ring_copy(q, n, owner, part, to):
        ref = (high_ref, low_ref)[q].at[owner, pl.ds(part * half, half)]
        return remote(ref, ref, ring_send.at[q, n], ring_recv.at[q, n], to)

    def twin_copy(q, n, owner):
        ref = (high_ref, low_ref)[q].at[owner]
        return remote(ref, ref, pair_send.at[q, n], pair_recv.at[q, n], twin)

    first = []
    for q in range(2):
        first.append((ring_copy(q, 0, cls, 0, right), ring_copy(q, 1, cls, 1, left),
                      ring_copy(q, 2, cls, 1, right), ring_copy(q, 3, cls, 0, left)))
        for copy in first[q]:
            copy.start()
    own = [twin_copy(q, 0, cls) for q in range(2)]
    for copy in own:
        copy.start()
    operate(2, copies)
    image_ref[...] = z_ref[...] - SHRINK * acc_ref[...]
    r_ref[...] = seed_ref[...] - image_ref[...]

    image_t = image_ref[...].T
    r_t = r_ref[...].T
    for n, value in enumerate((image_t, r_t)):
        top = value.astype(jnp.bfloat16)
        flat_ref[n * T:(n + 1) * T, :] = top
        flat_ref[(2 + n) * T:(3 + n) * T, :] = (value - top.astype(jnp.float32)).astype(jnp.bfloat16)

    second = []
    for q in range(2):
        first[q][0].wait_recv()
        a = ring_copy(q, 4, left_chip * 2 + core, 0, right)
        a.start()
        first[q][1].wait_recv()
        b = ring_copy(q, 5, right_chip * 2 + core, 1, left)
        b.start()
        second.append((a, b))
        first[q][2].wait_recv()
        c = twin_copy(q, 1, left_chip * 2 + core)
        c.start()
        first[q][3].wait_recv()
        d = twin_copy(q, 2, right_chip * 2 + core)
        d.start()
        own.extend((c, d))

    def grams(q, which):
        g = (high_ref, low_ref)[q]
        both = jnp.concatenate([g[which * 2], g[which * 2 + 1]], axis=1)
        at = pl.ds(pl.multiple_of(which * 2 * T, 2 * T), 2 * T)
        if q == 0:
            out = jnp.dot(flat_ref[...], both, preferred_element_type=jnp.float32)
            ct_ref[:, at] = out[0:T] + out[2 * T:3 * T]
            xt_ref[:, at] = out[T:2 * T] + out[3 * T:]
        else:
            out = jnp.dot(flat_ref[0:2 * T, :], both, preferred_element_type=jnp.float32)
            ct_ref[:, at] += out[0:T]
            xt_ref[:, at] += out[T:]

    for q in range(2):
        own[q].wait_recv()
        grams(q, chip)
    far = []
    for q in range(2):
        for copy in second[q]:
            copy.wait_recv()
        e = twin_copy(q, 3, far_chip * 2 + core)
        e.start()
        far.append(e)
        own[2 + 2 * q].wait_recv()
        grams(q, left_chip)
        own[3 + 2 * q].wait_recv()
        grams(q, right_chip)
    for q in range(2):
        far[q].wait_recv()
        grams(q, far_chip)
    for copy in list(copies) + list(first[0]) + list(first[1]) + list(second[0]) + list(second[1]) + own + far:
        copy.wait_send()


def find_direction(slots, weights, seed, tiles):
    rows, width = seed.shape
    every = lax.axis_size("cls")
    f32 = jnp.float32
    vmem = pl.BlockSpec(memory_space=pltpu.VMEM)
    smem = pl.BlockSpec(memory_space=pltpu.SMEM)
    sems = pltpu.SemaphoreType.DMA
    return pl.pallas_call(
        direction_kernel,
        out_shape=[
            jax.ShapeDtypeStruct((rows, width), f32),
            jax.ShapeDtypeStruct((rows, width), f32),
            jax.ShapeDtypeStruct((rows, width), f32),
            jax.ShapeDtypeStruct((every, rows, width), jnp.bfloat16),
            jax.ShapeDtypeStruct((width, every * width), f32),
            jax.ShapeDtypeStruct((width, every * width), f32),
        ],
        in_specs=[smem, smem, vmem, vmem],
        out_specs=[vmem] * 6,
        scratch_shapes=[
            pltpu.VMEM((3, rows + 16 * T, width), jnp.bfloat16),
            pltpu.VMEM((rows, width), f32),
            pltpu.VMEM((rows, width), f32),
            pltpu.VMEM((every, rows, width), jnp.bfloat16),
            pltpu.VMEM((4 * T, rows), jnp.bfloat16),
            sems((3, 2)), sems((3, 2)), sems((2, 6)), sems((2, 6)), sems((2, 4)), sems((2, 4)),
        ],
        compiler_params=pltpu.CompilerParams(collective_id=0, has_side_effects=True, vmem_limit_bytes=48 << 20),
    )(slots, weights, seed, tiles)


def by_offset(tile_cols, tile_count, tile_scale):
    local_blocks, slot_total = tile_cols.shape
    reach = (slot_total - 1) // 2
    total = local_blocks * lax.axis_size("node")
    row = jnp.arange(local_blocks)[:, None]
    where = jnp.mod(tile_cols - (lax.axis_index("node") * local_blocks + row) + reach, total)
    slot = jnp.arange(slot_total)[None, :]
    weights = jnp.where(slot < tile_count[:, None], tile_scale, 0.0)
    hit = where[:, :, None] == jnp.arange(slot_total)[None, None, :]
    slots = jnp.sum(jnp.where(hit, (row * slot_total + slot)[:, :, None], 0), axis=1)
    return slots.reshape(-1), jnp.sum(jnp.where(hit, weights[:, :, None], 0.0), axis=1).reshape(-1)


def sum_kernel(ct_ref, xt_ref, full_ref, xs_ref,
               first_ref, part_ref, second_ref,
               send1, recv1, send2, recv2, send_a, recv_a, send_b, recv_b, send_c, recv_c,
               send_t, recv_t, send_xb, recv_xb, send_xc, recv_xc):
    side = 4
    node, cls = lax.axis_index("node"), lax.axis_index("cls")
    chip, core = cls // 2, cls % 2
    y, z = node // side, node % side
    f = jnp.where(core == 0, z, y)
    s = jnp.where(core == 0, y, z)

    def at(f_, s_):
        return {"node": jnp.where(core == 0, s_ * side + f_, f_ * side + s_)}

    def turn(v, m):
        return (v + m) % side

    along_f = [at(turn(f, m), s) for m in range(1, side)]
    along_s = [at(f, turn(s, m)) for m in range(1, side)]
    along_x = [{"cls": turn(chip, m) * 2 + core} for m in range(1, side)]
    twin = {"cls": chip * 2 + 1 - core}
    greet(along_f + along_s + along_x + [twin])

    pending = []

    def go(copies):
        for copy in copies:
            copy.start()
        pending.extend(copies)
        return copies

    grams = (ct_ref, xt_ref)
    stage1 = [go([remote(grams[q].at[:, turn(f, m)], first_ref.at[q, m - 1],
                         send1.at[q, m - 1], recv1.at[q, m - 1], along_f[m - 1])
                  for m in range(1, side)]) for q in range(2)]
    stage2 = []
    for q in range(2):
        for copy in stage1[q]:
            copy.wait_recv()
        for k in range(side):
            part_ref[q, k] = (grams[q][k, f] + first_ref[q, 0, k]) + (first_ref[q, 1, k] + first_ref[q, 2, k])
        stage2.append(go([remote(part_ref.at[q, turn(s, m)], second_ref.at[q, m - 1],
                                 send2.at[q, m - 1], recv2.at[q, m - 1], along_s[m - 1])
                          for m in range(1, side)]))
    def finish(q):
        for copy in stage2[q]:
            copy.wait_recv()
        return (part_ref[q, s] + second_ref[q, 0]) + (second_ref[q, 1] + second_ref[q, 2])

    full_ref[chip, core, s, f] = finish(0)
    mine = full_ref.at[chip, core, s, f]
    stage_a = go([remote(mine, mine, send_a.at[m], recv_a.at[m], along_x[m]) for m in range(side - 1)])
    xs_ref[s, f] = finish(1)
    mine_x = xs_ref.at[s, f]
    stage_xb = go([remote(mine_x, mine_x, send_xb.at[m], recv_xb.at[m], along_f[m]) for m in range(side - 1)])
    for copy in stage_a:
        copy.wait_recv()
    line = full_ref.at[:, core, s, f]
    stage_b = go([remote(line, line, send_b.at[m], recv_b.at[m], along_f[m]) for m in range(side - 1)])
    for copy in stage_xb:
        copy.wait_recv()
    line_x = xs_ref.at[s]
    stage_xc = go([remote(line_x, line_x, send_xc.at[m], recv_xc.at[m], along_s[m]) for m in range(side - 1)])
    for copy in stage_b:
        copy.wait_recv()

    def slab(owner, h):
        return full_ref.at[pl.ds(2 * h, 2), core, owner]

    def ring(n, owner, h, to):
        return remote(slab(owner, h), slab(owner, h), send_c.at[n], recv_c.at[n], to)

    def share(n, owner, h):
        return remote(slab(owner, h), slab(owner, h), send_t.at[n], recv_t.at[n], twin)

    up, down = along_s[0], along_s[2]
    before, after, across = turn(s, 3), turn(s, 1), turn(s, 2)
    c0, c1, c2, c3 = go([ring(0, s, 0, up), ring(1, s, 1, down), ring(2, s, 1, up), ring(3, s, 0, down)])
    shared = go([share(0, s, 0), share(1, s, 1)])
    c0.wait_recv()
    fwd0, = go([ring(4, before, 0, up)])
    c1.wait_recv()
    fwd1, = go([ring(5, after, 1, down)])
    shared += go([share(2, before, 0), share(3, after, 1)])
    c2.wait_recv()
    shared += go([share(4, before, 1)])
    c3.wait_recv()
    shared += go([share(5, after, 0)])
    fwd0.wait_recv()
    shared += go([share(6, across, 0)])
    fwd1.wait_recv()
    shared += go([share(7, across, 1)])
    for copy in stage_xc + shared:
        copy.wait_recv()
    for copy in pending:
        copy.wait_send()


def sum_and_share(ct, xt):
    width, classes = ct.shape
    f32 = jnp.float32
    vmem = pl.BlockSpec(memory_space=pltpu.VMEM)
    sems = pltpu.SemaphoreType.DMA
    cut = (4, 4, width // 16, classes)
    full, xs = pl.pallas_call(
        sum_kernel,
        out_shape=[jax.ShapeDtypeStruct((4, 2) + cut, f32), jax.ShapeDtypeStruct(cut, f32)],
        in_specs=[vmem] * 2,
        out_specs=[vmem] * 2,
        scratch_shapes=[
            pltpu.VMEM((2, 3, 4, width // 16, classes), f32),
            pltpu.VMEM((2, 4, width // 16, classes), f32),
            pltpu.VMEM((2, 3, width // 16, classes), f32),
            sems((2, 3)), sems((2, 3)), sems((2, 3)), sems((2, 3)),
            sems((3,)), sems((3,)), sems((3,)), sems((3,)), sems((6,)), sems((6,)),
            sems((8,)), sems((8,)), sems((3,)), sems((3,)), sems((3,)), sems((3,)),
        ],
        compiler_params=pltpu.CompilerParams(collective_id=1, has_side_effects=True, vmem_limit_bytes=32 << 20),
    )(ct.reshape(cut), xt.reshape(cut))
    return full.reshape(classes, classes), xs.reshape(width, classes)


def dot(a, b, dims=((1,), (0,))):
    return lax.dot_general(a, b, (dims, ((), ())), precision=HI, preferred_element_type=jnp.float32)

def row_of(x, j):
    return jnp.broadcast_to(x[j:j + 1, :], (8, T))

def factor(rows):
    lane = lax.broadcasted_iota(jnp.int32, (8, T), 1)
    sub = lax.broadcasted_iota(jnp.int32, (8, T), 0)
    out = []
    for k in range(16):
        cols = [[jnp.broadcast_to(r[:, 8 * k + j:8 * k + j + 1], (8, T)) for j in range(8)] for r in rows[k:]]
        inside = (lane >= 8 * k) & (lane < 8 * k + 8)
        unit = jnp.where(lane - 8 * k == sub, 1.0, 0.0)
        panel = jnp.where(inside, unit, rows[k])
        b = list(cols[0])
        done = jnp.zeros((8, T), jnp.float32)
        for j in range(8):
            p = row_of(b[j], j)
            r = 1.0 / p
            f = b[j]
            own = sub == j
            top = row_of(panel, j)
            done = jnp.where(own, top * lax.rsqrt(p), done)
            n = top * r
            panel = jnp.where(own, n, panel - f * n)
            for l in range(j + 1, 8):
                n = row_of(b[l], j) * r
                b[l] = jnp.where(own, n, b[l] - f * n)
        out.append(jnp.where(lane < 8 * k + 8, done, 0.0))
        spread = [row_of(panel, j) for j in range(8)]
        for g in range(k + 1, 16):
            acc = jnp.where(inside, 0.0, rows[g])
            for j in range(8):
                acc = acc - cols[g - k][j] * spread[j]
            rows[g] = acc
    return out

def solve_kernel(c_ref, x_ref, z_ref, a_ref, l_ref, v_ref):
    n = c_ref.shape[0]
    nb = n // T
    for i in range(nb):
        for j in range(i, nb):
            a_ref[i * T:(i + 1) * T, j * T:(j + 1) * T] = 0.5 * (
                c_ref[i * T:(i + 1) * T, j * T:(j + 1) * T] + c_ref[j * T:(j + 1) * T, i * T:(i + 1) * T].T)
    a_ref[:, n:] = x_ref[...]

    def step(k, _):
        base = pl.multiple_of(k * T, T)
        here = pl.ds(base, T)
        rows = [a_ref[pl.ds(base + 8 * g, 8), here] for g in range(16)]
        rows = factor(rows)
        for g in range(16):
            l_ref[pl.ds(base + 8 * g, 8), :] = rows[g]
        v_ref[here, :] = dot(l_ref[here, :], a_ref[here, :])
        def trail(i, _):
            at = pl.multiple_of(i * T, T)
            a_ref[pl.ds(at, T), :] -= dot(v_ref[here, pl.ds(at, T)], v_ref[here, :], ((0,), (0,)))
            return 0
        lax.fori_loop(k + 1, nb, trail, 0)
        return 0
    lax.fori_loop(0, nb, step, 0)
    def back(s, _):
        j = nb - 1 - s
        at = pl.multiple_of(j * T, T)
        known = dot(l_ref[pl.ds(at, T), :], v_ref[pl.ds(at, T), n:], ((0,), (0,)))
        z_ref[pl.ds(at, T), :] = known
        def one(i, _):
            to = pl.multiple_of(i * T, T)
            v_ref[pl.ds(to, T), n:] -= dot(v_ref[pl.ds(to, T), pl.ds(at, T)], known)
            return 0
        lax.fori_loop(0, j, one, 0)
        return 0
    lax.fori_loop(0, nb, back, 0)

def solve(c, x):
    n = c.shape[0]
    return pl.pallas_call(
        solve_kernel,
        out_shape=jax.ShapeDtypeStruct(x.shape, jnp.float32),
        in_specs=[pl.BlockSpec(memory_space=pltpu.VMEM)] * 2,
        out_specs=pl.BlockSpec(memory_space=pltpu.VMEM),
        scratch_shapes=[pltpu.VMEM((n, n + T), jnp.float32), pltpu.VMEM((n, T), jnp.float32),
                        pltpu.VMEM((n, n + T), jnp.float32)],
        compiler_params=pltpu.CompilerParams(vmem_limit_bytes=40 << 20),
    )(c, x)
def body(seed_scores, tile_vals, tile_cols, tile_count, tile_scale):
    slots, weights = by_offset(tile_cols, tile_count, tile_scale)
    tiles = tile_vals.reshape(-1, T, T)
    direction, misfit, imaged, high, ct, xt = find_direction(slots, weights, seed_scores, tiles)
    all_imaged = lax.all_gather(imaged, "cls", axis=1, tiled=True)
    full, xt = sum_and_share(ct, xt)
    start = lax.axis_index("cls") * T
    mine = lax.dynamic_slice_in_dim(full, start, T, 1)
    own = lax.dynamic_slice_in_dim(full, start, T, 0)
    rhs = (xt + 0.5 * (own - mine.T)).T
    change = solve(full, rhs)
    packed = change.astype(jnp.bfloat16)
    mixed = sum(jnp.dot(high[n], packed[n * T:(n + 1) * T], preferred_element_type=jnp.float32) for n in range(high.shape[0]))
    solution = direction + mixed
    residual = misfit - jnp.dot(all_imaged, change, precision=HI)
    return (solution, residual)
def solution(mesh):
    return jax.shard_map(
        body,
        mesh=mesh,
        in_specs=(
            P("node", "cls"),
            P("node", None, None, None),
            P("node", None),
            P("node"),
            P("node", None),
        ),
        out_specs=(P("node", "cls"), P("node", "cls")),
        check_vma=False,
    )
```

```python
import functools
import jax
import jax.numpy as jnp
from jax import lax
from jax.experimental import pallas as pl
from jax.experimental.pallas import tpu as pltpu
from jax.sharding import PartitionSpec as P

SHRINK = 0.9
HI = lax.Precision.HIGHEST
MESH = pl.DeviceIdType.MESH
T = 128


def remote(src, dst, send, recv, to):
    return pltpu.make_async_remote_copy(
        src_ref=src, dst_ref=dst, send_sem=send, recv_sem=recv, device_id=to, device_id_type=MESH)


def greet(peers):
    barrier = pltpu.get_barrier_semaphore()
    for peer in peers:
        pl.semaphore_signal(barrier, inc=1, device_id=peer, device_id_type=MESH)
    pl.semaphore_wait(barrier, len(peers))


def direction_kernel(slot_ref, weight_ref, seed_ref, tiles_ref,
                     d_ref, r_ref, parts_ref, high_ref, ct_ref, xt_ref,
                     ext_ref, acc_ref, z_ref, low_ref, flat_ref,
                     halo_send, halo_recv, ring_send, ring_recv, pair_send, pair_recv):
    blocks = acc_ref.shape[0] // T
    reach = 8
    rows = blocks * T
    half = rows // 2
    edge = reach * T
    node, cls = lax.axis_index("node"), lax.axis_index("cls")
    nodes = lax.axis_size("node")
    chips = lax.axis_size("cls") // 2
    chip, core = cls // 2, cls % 2
    right_node, left_node = {"node": (node + 1) % nodes}, {"node": (node + nodes - 1) % nodes}
    right_chip, left_chip, far_chip = (chip + 1) % chips, (chip + chips - 1) % chips, (chip + 2) % chips
    right, left, twin = {"cls": right_chip * 2 + core}, {"cls": left_chip * 2 + core}, {"cls": chip * 2 + 1 - core}
    greet([right_node, left_node, right, left, twin])

    def halo_copies(s):
        ext = ext_ref.at[s]
        return (
            remote(ext.at[pl.ds(rows, edge)], ext.at[pl.ds(0, edge)],
                   halo_send.at[s, 0], halo_recv.at[s, 0], right_node),
            remote(ext.at[pl.ds(edge, edge)], ext.at[pl.ds(edge + rows, edge)],
                   halo_send.at[s, 1], halo_recv.at[s, 1], left_node),
        )

    def product(s, tile, source):
        return jnp.dot(tiles_ref[tile], ext_ref[s, pl.ds(pl.multiple_of(source * T, T), T), :],
                       preferred_element_type=jnp.float32)

    def spread(s, z):
        ext_ref[s, edge:edge + rows, :] = z.astype(jnp.bfloat16)
        copies = halo_copies(s)
        for copy in copies:
            copy.start()
        return copies

    def local_part(s):
        def one(i, _):
            total = jnp.zeros((T, T), jnp.float32)
            for j in range(blocks):
                o = j + reach - i
                fits = (o >= 0) & (o <= 2 * reach)
                at = i * (2 * reach + 1) + jnp.clip(o, 0, 2 * reach)
                w = jnp.where(fits, weight_ref[at], 0.0)
                total += w * product(s, slot_ref[at], j + reach)
            acc_ref[pl.ds(pl.multiple_of(i * T, T), T), :] = total
            return 0
        lax.fori_loop(0, blocks, one, 0)

    def edge_part(s):
        def one(t, _):
            low = jnp.zeros((T, T), jnp.float32)
            high = jnp.zeros((T, T), jnp.float32)
            for m in range(reach + 1):
                lower = m < reach - t
                i = jnp.where(lower, t, t + blocks - reach)
                j = t + m + jnp.where(lower, 0, blocks)
                at = i * (2 * reach + 1) + j - i
                w = weight_ref[at]
                p = product(s, slot_ref[at], j)
                low += jnp.where(lower, w, 0.0) * p
                high += jnp.where(lower, 0.0, w) * p
            acc_ref[pl.ds(pl.multiple_of(t * T, T), T), :] += low
            acc_ref[pl.ds(pl.multiple_of((t + blocks - reach) * T, T), T), :] += high
            return 0
        lax.fori_loop(0, reach, one, 0)

    def operate(s, copies):
        local_part(s)
        for copy in copies:
            copy.wait_recv()
        edge_part(s)

    factor = SHRINK
    z_ref[...] = seed_ref[...]
    d_ref[...] = seed_ref[...]
    for s in range(2):
        copies = spread(s, z_ref[...])
        operate(s, copies)
        factor_next = 1.0 / (2.0 / SHRINK - factor)
        misfit = seed_ref[...] - (z_ref[...] - SHRINK * acc_ref[...])
        update = factor_next * factor * d_ref[...] + (2.0 * factor_next / SHRINK) * misfit
        d_ref[...] = update
        z_ref[...] = z_ref[...] + update
        factor = factor_next
        for copy in copies:
            copy.wait_send()
    z = z_ref[...]
    d_ref[...] = z
    high = z.astype(jnp.bfloat16)
    high_ref[cls] = high
    low_ref[cls] = (z - high.astype(jnp.float32)).astype(jnp.bfloat16)
    copies = spread(2, z)

    def ring_copy(q, n, owner, part, to):
        ref = (high_ref, low_ref)[q].at[owner, pl.ds(part * half, half)]
        return remote(ref, ref, ring_send.at[q, n], ring_recv.at[q, n], to)

    def twin_copy(q, n, owner):
        ref = (high_ref, low_ref)[q].at[owner]
        return remote(ref, ref, pair_send.at[q, n], pair_recv.at[q, n], twin)

    first = []
    for q in range(2):
        first.append((ring_copy(q, 0, cls, 0, right), ring_copy(q, 1, cls, 1, left),
                      ring_copy(q, 2, cls, 1, right), ring_copy(q, 3, cls, 0, left)))
        for copy in first[q]:
            copy.start()
    own = [twin_copy(q, 0, cls) for q in range(2)]
    for copy in own:
        copy.start()
    operate(2, copies)
    image = z_ref[...] - SHRINK * acc_ref[...]
    r_ref[...] = seed_ref[...] - image
    coarse = image.astype(jnp.bfloat16)
    parts_ref[0:rows, :] = coarse
    parts_ref[rows:, :] = (image - coarse.astype(jnp.float32)).astype(jnp.bfloat16)

    image_t = image.T
    r_t = r_ref[...].T
    for n, value in enumerate((image_t, r_t)):
        top = value.astype(jnp.bfloat16)
        flat_ref[n * T:(n + 1) * T, :] = top
        flat_ref[(2 + n) * T:(3 + n) * T, :] = (value - top.astype(jnp.float32)).astype(jnp.bfloat16)

    second = []
    for q in range(2):
        first[q][0].wait_recv()
        a = ring_copy(q, 4, left_chip * 2 + core, 0, right)
        a.start()
        first[q][1].wait_recv()
        b = ring_copy(q, 5, right_chip * 2 + core, 1, left)
        b.start()
        second.append((a, b))
        first[q][2].wait_recv()
        c = twin_copy(q, 1, left_chip * 2 + core)
        c.start()
        first[q][3].wait_recv()
        d = twin_copy(q, 2, right_chip * 2 + core)
        d.start()
        own.extend((c, d))

    def grams(q, which):
        g = (high_ref, low_ref)[q]
        both = jnp.concatenate([g[which * 2], g[which * 2 + 1]], axis=1)
        at = pl.ds(pl.multiple_of(which * 2 * T, 2 * T), 2 * T)
        if q == 0:
            out = jnp.dot(flat_ref[...], both, preferred_element_type=jnp.float32)
            ct_ref[:, at] = out[0:T] + out[2 * T:3 * T]
            xt_ref[:, at] = out[T:2 * T] + out[3 * T:]
        else:
            out = jnp.dot(flat_ref[0:2 * T, :], both, preferred_element_type=jnp.float32)
            ct_ref[:, at] += out[0:T]
            xt_ref[:, at] += out[T:]

    for q in range(2):
        own[q].wait_recv()
        grams(q, chip)
    far = []
    for q in range(2):
        for copy in second[q]:
            copy.wait_recv()
        e = twin_copy(q, 3, far_chip * 2 + core)
        e.start()
        far.append(e)
        own[2 + 2 * q].wait_recv()
        grams(q, left_chip)
        own[3 + 2 * q].wait_recv()
        grams(q, right_chip)
    for q in range(2):
        far[q].wait_recv()
        grams(q, far_chip)
    for copy in list(copies) + list(first[0]) + list(first[1]) + list(second[0]) + list(second[1]) + own + far:
        copy.wait_send()


def find_direction(slots, weights, seed, tiles):
    rows, width = seed.shape
    every = lax.axis_size("cls")
    f32 = jnp.float32
    vmem = pl.BlockSpec(memory_space=pltpu.VMEM)
    smem = pl.BlockSpec(memory_space=pltpu.SMEM)
    sems = pltpu.SemaphoreType.DMA
    return pl.pallas_call(
        direction_kernel,
        out_shape=[
            jax.ShapeDtypeStruct((rows, width), f32),
            jax.ShapeDtypeStruct((rows, width), f32),
            jax.ShapeDtypeStruct((2 * rows, width), jnp.bfloat16),
            jax.ShapeDtypeStruct((every, rows, width), jnp.bfloat16),
            jax.ShapeDtypeStruct((width, every * width), f32),
            jax.ShapeDtypeStruct((width, every * width), f32),
        ],
        in_specs=[smem, smem, vmem, vmem],
        out_specs=[vmem] * 6,
        scratch_shapes=[
            pltpu.VMEM((3, rows + 16 * T, width), jnp.bfloat16),
            pltpu.VMEM((rows, width), f32),
            pltpu.VMEM((rows, width), f32),
            pltpu.VMEM((every, rows, width), jnp.bfloat16),
            pltpu.VMEM((4 * T, rows), jnp.bfloat16),
            sems((3, 2)), sems((3, 2)), sems((2, 6)), sems((2, 6)), sems((2, 4)), sems((2, 4)),
        ],
        compiler_params=pltpu.CompilerParams(collective_id=0, has_side_effects=True, vmem_limit_bytes=48 << 20),
    )(slots, weights, seed, tiles)


def by_offset(tile_cols, tile_count, tile_scale):
    local_blocks, slot_total = tile_cols.shape
    reach = (slot_total - 1) // 2
    total = local_blocks * lax.axis_size("node")
    row = jnp.arange(local_blocks)[:, None]
    where = jnp.mod(tile_cols - (lax.axis_index("node") * local_blocks + row) + reach, total)
    slot = jnp.arange(slot_total)[None, :]
    weights = jnp.where(slot < tile_count[:, None], tile_scale, 0.0)
    hit = where[:, :, None] == jnp.arange(slot_total)[None, None, :]
    slots = jnp.sum(jnp.where(hit, (row * slot_total + slot)[:, :, None], 0), axis=1)
    return slots.reshape(-1), jnp.sum(jnp.where(hit, weights[:, :, None], 0.0), axis=1).reshape(-1)


def sum_kernel(ct_ref, xt_ref, full_ref, xs_ref,
               first_ref, part_ref, second_ref,
               send1, recv1, send2, recv2, send_a, recv_a, send_b, recv_b, send_c, recv_c,
               send_t, recv_t, send_xb, recv_xb, send_xc, recv_xc):
    side = 4
    node, cls = lax.axis_index("node"), lax.axis_index("cls")
    chip, core = cls // 2, cls % 2
    y, z = node // side, node % side
    f = jnp.where(core == 0, z, y)
    s = jnp.where(core == 0, y, z)

    def at(f_, s_):
        return {"node": jnp.where(core == 0, s_ * side + f_, f_ * side + s_)}

    def turn(v, m):
        return (v + m) % side

    along_f = [at(turn(f, m), s) for m in range(1, side)]
    along_s = [at(f, turn(s, m)) for m in range(1, side)]
    along_x = [{"cls": turn(chip, m) * 2 + core} for m in range(1, side)]
    twin = {"cls": chip * 2 + 1 - core}
    greet(along_f + along_s + along_x + [twin])

    pending = []

    def go(copies):
        for copy in copies:
            copy.start()
        pending.extend(copies)
        return copies

    grams = (ct_ref, xt_ref)
    stage1 = [go([remote(grams[q].at[:, turn(f, m)], first_ref.at[q, m - 1],
                         send1.at[q, m - 1], recv1.at[q, m - 1], along_f[m - 1])
                  for m in range(1, side)]) for q in range(2)]
    stage2 = []
    for q in range(2):
        for copy in stage1[q]:
            copy.wait_recv()
        for k in range(side):
            part_ref[q, k] = (grams[q][k, f] + first_ref[q, 0, k]) + (first_ref[q, 1, k] + first_ref[q, 2, k])
        stage2.append(go([remote(part_ref.at[q, turn(s, m)], second_ref.at[q, m - 1],
                                 send2.at[q, m - 1], recv2.at[q, m - 1], along_s[m - 1])
                          for m in range(1, side)]))
    def finish(q):
        for copy in stage2[q]:
            copy.wait_recv()
        return (part_ref[q, s] + second_ref[q, 0]) + (second_ref[q, 1] + second_ref[q, 2])

    full_ref[chip, core, s, f] = finish(0)
    mine = full_ref.at[chip, core, s, f]
    stage_a = go([remote(mine, mine, send_a.at[m], recv_a.at[m], along_x[m]) for m in range(side - 1)])
    xs_ref[s, f] = finish(1)
    mine_x = xs_ref.at[s, f]
    stage_xb = go([remote(mine_x, mine_x, send_xb.at[m], recv_xb.at[m], along_f[m]) for m in range(side - 1)])
    for copy in stage_a:
        copy.wait_recv()
    line = full_ref.at[:, core, s, f]
    stage_b = go([remote(line, line, send_b.at[m], recv_b.at[m], along_f[m]) for m in range(side - 1)])
    for copy in stage_xb:
        copy.wait_recv()
    line_x = xs_ref.at[s]
    stage_xc = go([remote(line_x, line_x, send_xc.at[m], recv_xc.at[m], along_s[m]) for m in range(side - 1)])
    for copy in stage_b:
        copy.wait_recv()

    def slab(owner, h):
        return full_ref.at[pl.ds(2 * h, 2), core, owner]

    def ring(n, owner, h, to):
        return remote(slab(owner, h), slab(owner, h), send_c.at[n], recv_c.at[n], to)

    def share(n, owner, h):
        return remote(slab(owner, h), slab(owner, h), send_t.at[n], recv_t.at[n], twin)

    up, down = along_s[0], along_s[2]
    before, after, across = turn(s, 3), turn(s, 1), turn(s, 2)
    c0, c1, c2, c3 = go([ring(0, s, 0, up), ring(1, s, 1, down), ring(2, s, 1, up), ring(3, s, 0, down)])
    shared = go([share(0, s, 0), share(1, s, 1)])
    c0.wait_recv()
    fwd0, = go([ring(4, before, 0, up)])
    c1.wait_recv()
    fwd1, = go([ring(5, after, 1, down)])
    shared += go([share(2, before, 0), share(3, after, 1)])
    c2.wait_recv()
    shared += go([share(4, before, 1)])
    c3.wait_recv()
    shared += go([share(5, after, 0)])
    fwd0.wait_recv()
    shared += go([share(6, across, 0)])
    fwd1.wait_recv()
    shared += go([share(7, across, 1)])
    for copy in stage_xc + shared:
        copy.wait_recv()
    for copy in pending:
        copy.wait_send()


def sum_and_share(ct, xt):
    width, classes = ct.shape
    f32 = jnp.float32
    vmem = pl.BlockSpec(memory_space=pltpu.VMEM)
    sems = pltpu.SemaphoreType.DMA
    cut = (4, 4, width // 16, classes)
    full, xs = pl.pallas_call(
        sum_kernel,
        out_shape=[jax.ShapeDtypeStruct((4, 2) + cut, f32), jax.ShapeDtypeStruct(cut, f32)],
        in_specs=[vmem] * 2,
        out_specs=[vmem] * 2,
        scratch_shapes=[
            pltpu.VMEM((2, 3, 4, width // 16, classes), f32),
            pltpu.VMEM((2, 4, width // 16, classes), f32),
            pltpu.VMEM((2, 3, width // 16, classes), f32),
            sems((2, 3)), sems((2, 3)), sems((2, 3)), sems((2, 3)),
            sems((3,)), sems((3,)), sems((3,)), sems((3,)), sems((6,)), sems((6,)),
            sems((8,)), sems((8,)), sems((3,)), sems((3,)), sems((3,)), sems((3,)),
        ],
        compiler_params=pltpu.CompilerParams(collective_id=1, has_side_effects=True, vmem_limit_bytes=32 << 20),
    )(ct.reshape(cut), xt.reshape(cut))
    return full.reshape(classes, classes), xs.reshape(width, classes)


ND = 2

def dot(a, b, dims=((1,), (0,))):
    return lax.dot_general(a, b, (dims, ((), ())), precision=HI, preferred_element_type=jnp.float32)

def row_of(x, j):
    return jnp.broadcast_to(x[j:j + 1, :], (8, T))

def factor(rows):
    lane = lax.broadcasted_iota(jnp.int32, (8, T), 1)
    sub = lax.broadcasted_iota(jnp.int32, (8, T), 0)
    own = [sub == j for j in range(8)]
    out = []

    def splat(x, c):
        return jnp.broadcast_to(x[:, c:c + 1], (8, T))

    ahead = [splat(rows[0], c) for c in range(8)]
    for k in range(16):
        last = k == 15
        inside = (lane >= 8 * k) & (lane < 8 * k + 8)
        b = ahead
        later = [] if last else [splat(rows[k], 8 * k + 8 + c) for c in range(8)]
        cols = [[splat(r, 8 * k + j) for j in range(8)] for r in rows[k + 1:k + 1 + ND]]
        fresh = [] if last else [splat(rows[k + 1], 8 * k + 8 + c) for c in range(8)]
        panel = jnp.where(inside, jnp.where(lane - 8 * k == sub, 1.0, 0.0), rows[k])
        done = jnp.zeros((8, T), jnp.float32)
        for j in range(8):
            p = row_of(b[j], j)
            r = 1.0 / p
            f = b[j]

            def clear(x):
                n = row_of(x, j) * r
                return jnp.where(own[j], n, x - f * n)

            done = jnp.where(own[j], row_of(panel, j) * lax.rsqrt(p), done)
            for l in range(j + 1, 8):
                b[l] = clear(b[l])
            later = [clear(x) for x in later]
            panel = clear(panel)
        out.append(jnp.where(lane < 8 * k + 8, done, 0.0))
        if last:
            break
        ahead = []
        for c in range(8):
            terms = [cols[0][j] * row_of(later[c], j) for j in range(8)]
            while len(terms) > 1:
                terms = [terms[i] + terms[i + 1] for i in range(0, len(terms), 2)]
            ahead.append(fresh[c] - terms[0])
        spread = [row_of(panel, j) for j in range(8)]
        near = min(k + 1 + ND, 16)
        if near < 16:
            wide = [jnp.zeros((8, T), jnp.float32)] * 16
            wide[k] = panel
            away = dot(jnp.concatenate(rows[near:], axis=0), jnp.concatenate(wide, axis=0))
        for g in range(k + 1, 16):
            acc = jnp.where(inside, 0.0, rows[g])
            if g < near:
                for j in range(8):
                    acc = acc - cols[g - k - 1][j] * spread[j]
            else:
                acc = acc - away[8 * (g - near):8 * (g - near) + 8]
            rows[g] = acc
    return out

def solve_kernel(c_ref, x_ref, z_ref, a_ref, l_ref, v_ref):
    n = c_ref.shape[0]
    nb = n // T
    wide = n + T
    for i in range(nb):
        for j in range(i, nb):
            a_ref[i * T:(i + 1) * T, j * T:(j + 1) * T] = 0.5 * (
                c_ref[i * T:(i + 1) * T, j * T:(j + 1) * T] + c_ref[j * T:(j + 1) * T, i * T:(i + 1) * T].T)
    start = pl.multiple_of(lax.axis_index("cls") * T, T)
    for i in range(nb):
        here = slice(i * T, (i + 1) * T)
        a_ref[here, n:] = (x_ref[:, here] + 0.5 * c_ref[pl.ds(start, T), here]).T - 0.5 * c_ref[here, pl.ds(start, T)]
    def update(k, i):
        here, there = slice(k * T, (k + 1) * T), slice(i * T, (i + 1) * T)
        a_ref[there, i * T:] -= dot(v_ref[here, there], v_ref[here, i * T:], ((0,), (0,)))

    for k in range(nb):
        here = slice(k * T, (k + 1) * T)
        rows = factor([a_ref[k * T + 8 * g:k * T + 8 * g + 8, here] for g in range(16)])
        for i in range(k + 1, nb):
            if k:
                update(k - 1, i)
        for g in range(16):
            l_ref[k * T + 8 * g:k * T + 8 * g + 8, :] = rows[g]
        v_ref[here, (k + 1) * T:] = dot(l_ref[here, :], a_ref[here, (k + 1) * T:])
        if k + 1 < nb:
            update(k, k + 1)
    y = v_ref[:, n:]
    for j in range(nb - 1, -1, -1):
        here = slice(j * T, (j + 1) * T)
        known = dot(l_ref[here, :], y[here], ((0,), (0,)))
        z_ref[here, :] = known
        if j:
            y = y[:j * T] - dot(v_ref[:j * T, here], known)

def solve(c, x):
    n = c.shape[0]
    return pl.pallas_call(
        solve_kernel,
        out_shape=jax.ShapeDtypeStruct((n, T), jnp.float32),
        in_specs=[pl.BlockSpec(memory_space=pltpu.VMEM)] * 2,
        out_specs=pl.BlockSpec(memory_space=pltpu.VMEM),
        scratch_shapes=[pltpu.VMEM((n, n + T), jnp.float32), pltpu.VMEM((n, T), jnp.float32),
                        pltpu.VMEM((n, n + T), jnp.float32)],
        compiler_params=pltpu.CompilerParams(vmem_limit_bytes=40 << 20),
    )(c, x)


def body(seed_scores, tile_vals, tile_cols, tile_count, tile_scale):
    slots, weights = by_offset(tile_cols, tile_count, tile_scale)
    tiles = tile_vals.reshape(-1, T, T)
    direction, misfit, parts, high, ct, xt = find_direction(slots, weights, seed_scores, tiles)
    all_parts = lax.all_gather(parts, "cls", axis=1, tiled=True)
    full, xs = sum_and_share(ct, xt)
    change = solve(full, xs)
    rows = direction.shape[0]
    top = change.astype(jnp.bfloat16)
    rest = (change - top.astype(jnp.float32)).astype(jnp.bfloat16)

    def times(a, b):
        return jnp.dot(a, b, preferred_element_type=jnp.float32)

    mixed = sum(times(high[n], top[n * T:(n + 1) * T]) for n in range(high.shape[0]))
    coarse, fine = all_parts[:rows], all_parts[rows:]
    residual = misfit - (times(coarse, top) + (times(coarse, rest) + times(fine, top)))
    return (direction + mixed, residual)


def solution(mesh):
    return jax.shard_map(
        body,
        mesh=mesh,
        in_specs=(
            P("node", "cls"),
            P("node", None, None, None),
            P("node", None),
            P("node"),
            P("node", None),
        ),
        out_specs=(P("node", "cls"), P("node", "cls")),
        check_vma=False,
    )
```

```python
import functools
import jax
import jax.numpy as jnp
from jax import lax
from jax.experimental import pallas as pl
from jax.experimental.pallas import tpu as pltpu
from jax.sharding import PartitionSpec as P

SHRINK = 0.9
HI = lax.Precision.HIGHEST
MESH = pl.DeviceIdType.MESH
T = 128


def remote(src, dst, send, recv, to):
    return pltpu.make_async_remote_copy(
        src_ref=src, dst_ref=dst, send_sem=send, recv_sem=recv, device_id=to, device_id_type=MESH)


def greet(peers):
    barrier = pltpu.get_barrier_semaphore()
    for peer in peers:
        pl.semaphore_signal(barrier, inc=1, device_id=peer, device_id_type=MESH)
    pl.semaphore_wait(barrier, len(peers))


def direction_kernel(slot_ref, weight_ref, seed_ref, tiles_hbm,
                     d_ref, r_ref, parts_ref, high_ref, ct_ref, xt_ref,
                     tiles_ref, ext_ref, acc_ref, z_ref, low_ref, flat_ref, tiles_sem,
                     halo_send, halo_recv, ring_send, ring_recv, pair_send, pair_recv):
    fetch = pltpu.make_async_copy(tiles_hbm, tiles_ref, tiles_sem)
    fetch.start()
    blocks = acc_ref.shape[0] // T
    reach = 8
    rows = blocks * T
    half = rows // 2
    edge = reach * T
    node, cls = lax.axis_index("node"), lax.axis_index("cls")
    nodes = lax.axis_size("node")
    chips = lax.axis_size("cls") // 2
    chip, core = cls // 2, cls % 2
    right_node, left_node = {"node": (node + 1) % nodes}, {"node": (node + nodes - 1) % nodes}
    right_chip, left_chip, far_chip = (chip + 1) % chips, (chip + chips - 1) % chips, (chip + 2) % chips
    right, left, twin = {"cls": right_chip * 2 + core}, {"cls": left_chip * 2 + core}, {"cls": chip * 2 + 1 - core}
    greet([right_node, left_node, right, left, twin])

    def halo_copies(s):
        ext = ext_ref.at[s]
        return (
            remote(ext.at[pl.ds(rows, edge)], ext.at[pl.ds(0, edge)],
                   halo_send.at[s, 0], halo_recv.at[s, 0], right_node),
            remote(ext.at[pl.ds(edge, edge)], ext.at[pl.ds(edge + rows, edge)],
                   halo_send.at[s, 1], halo_recv.at[s, 1], left_node),
        )

    def product(s, tile, source):
        return jnp.dot(tiles_ref[tile], ext_ref[s, pl.ds(pl.multiple_of(source * T, T), T), :],
                       preferred_element_type=jnp.float32)

    def spread(s, z):
        ext_ref[s, edge:edge + rows, :] = z.astype(jnp.bfloat16)
        copies = halo_copies(s)
        for copy in copies:
            copy.start()
        return copies

    def local_part(s):
        def one(i, _):
            total = jnp.zeros((T, T), jnp.float32)
            for j in range(blocks):
                o = j + reach - i
                fits = (o >= 0) & (o <= 2 * reach)
                at = i * (2 * reach + 1) + jnp.clip(o, 0, 2 * reach)
                w = jnp.where(fits, weight_ref[at], 0.0)
                total += w * product(s, slot_ref[at], j + reach)
            acc_ref[pl.ds(pl.multiple_of(i * T, T), T), :] = total
            return 0
        lax.fori_loop(0, blocks, one, 0)

    def edge_part(s):
        def one(t, _):
            low = jnp.zeros((T, T), jnp.float32)
            high = jnp.zeros((T, T), jnp.float32)
            for m in range(reach + 1):
                lower = m < reach - t
                i = jnp.where(lower, t, t + blocks - reach)
                j = t + m + jnp.where(lower, 0, blocks)
                at = i * (2 * reach + 1) + j - i
                w = weight_ref[at]
                p = product(s, slot_ref[at], j)
                low += jnp.where(lower, w, 0.0) * p
                high += jnp.where(lower, 0.0, w) * p
            acc_ref[pl.ds(pl.multiple_of(t * T, T), T), :] += low
            acc_ref[pl.ds(pl.multiple_of((t + blocks - reach) * T, T), T), :] += high
            return 0
        lax.fori_loop(0, reach, one, 0)

    def operate(s, copies):
        local_part(s)
        for copy in copies:
            copy.wait_recv()
        edge_part(s)

    factor = SHRINK
    z_ref[...] = seed_ref[...]
    d_ref[...] = seed_ref[...]
    for s in range(2):
        copies = spread(s, z_ref[...])
        if s == 0:
            fetch.wait()
        operate(s, copies)
        factor_next = 1.0 / (2.0 / SHRINK - factor)
        misfit = seed_ref[...] - (z_ref[...] - SHRINK * acc_ref[...])
        update = factor_next * factor * d_ref[...] + (2.0 * factor_next / SHRINK) * misfit
        d_ref[...] = update
        z_ref[...] = z_ref[...] + update
        factor = factor_next
        for copy in copies:
            copy.wait_send()
    z = z_ref[...]
    d_ref[...] = z
    high = z.astype(jnp.bfloat16)
    high_ref[cls] = high
    low_ref[cls] = (z - high.astype(jnp.float32)).astype(jnp.bfloat16)
    copies = spread(2, z)

    def ring_copy(q, n, owner, part, to):
        ref = (high_ref, low_ref)[q].at[owner, pl.ds(part * half, half)]
        return remote(ref, ref, ring_send.at[q, n], ring_recv.at[q, n], to)

    def twin_copy(q, n, owner):
        ref = (high_ref, low_ref)[q].at[owner]
        return remote(ref, ref, pair_send.at[q, n], pair_recv.at[q, n], twin)

    first = []
    for q in range(2):
        first.append((ring_copy(q, 0, cls, 0, right), ring_copy(q, 1, cls, 1, left),
                      ring_copy(q, 2, cls, 1, right), ring_copy(q, 3, cls, 0, left)))
        for copy in first[q]:
            copy.start()
    own = [twin_copy(q, 0, cls) for q in range(2)]
    for copy in own:
        copy.start()
    operate(2, copies)
    image = z_ref[...] - SHRINK * acc_ref[...]
    r_ref[...] = seed_ref[...] - image
    coarse = image.astype(jnp.bfloat16)
    parts_ref[0:rows, :] = coarse
    parts_ref[rows:, :] = (image - coarse.astype(jnp.float32)).astype(jnp.bfloat16)

    image_t = image.T
    r_t = r_ref[...].T
    for n, value in enumerate((image_t, r_t)):
        top = value.astype(jnp.bfloat16)
        flat_ref[n * T:(n + 1) * T, :] = top
        flat_ref[(2 + n) * T:(3 + n) * T, :] = (value - top.astype(jnp.float32)).astype(jnp.bfloat16)

    second = []
    for q in range(2):
        first[q][0].wait_recv()
        a = ring_copy(q, 4, left_chip * 2 + core, 0, right)
        a.start()
        first[q][1].wait_recv()
        b = ring_copy(q, 5, right_chip * 2 + core, 1, left)
        b.start()
        second.append((a, b))
        first[q][2].wait_recv()
        c = twin_copy(q, 1, left_chip * 2 + core)
        c.start()
        first[q][3].wait_recv()
        d = twin_copy(q, 2, right_chip * 2 + core)
        d.start()
        own.extend((c, d))

    def grams(q, which):
        g = (high_ref, low_ref)[q]
        both = jnp.concatenate([g[which * 2], g[which * 2 + 1]], axis=1)
        at = pl.ds(pl.multiple_of(which * 2 * T, 2 * T), 2 * T)
        if q == 0:
            out = jnp.dot(flat_ref[...], both, preferred_element_type=jnp.float32)
            ct_ref[:, at] = out[0:T] + out[2 * T:3 * T]
            xt_ref[:, at] = out[T:2 * T] + out[3 * T:]
        else:
            out = jnp.dot(flat_ref[0:2 * T, :], both, preferred_element_type=jnp.float32)
            ct_ref[:, at] += out[0:T]
            xt_ref[:, at] += out[T:]

    for q in range(2):
        own[q].wait_recv()
        grams(q, chip)
    far = []
    for q in range(2):
        for copy in second[q]:
            copy.wait_recv()
        e = twin_copy(q, 3, far_chip * 2 + core)
        e.start()
        far.append(e)
        own[2 + 2 * q].wait_recv()
        grams(q, left_chip)
        own[3 + 2 * q].wait_recv()
        grams(q, right_chip)
    for q in range(2):
        far[q].wait_recv()
        grams(q, far_chip)
    for copy in list(copies) + list(first[0]) + list(first[1]) + list(second[0]) + list(second[1]) + own + far:
        copy.wait_send()


def find_direction(slots, weights, seed, tiles):
    rows, width = seed.shape
    every = lax.axis_size("cls")
    f32 = jnp.float32
    vmem = pl.BlockSpec(memory_space=pltpu.VMEM)
    smem = pl.BlockSpec(memory_space=pltpu.SMEM)
    sems = pltpu.SemaphoreType.DMA
    return pl.pallas_call(
        direction_kernel,
        out_shape=[
            jax.ShapeDtypeStruct((rows, width), f32),
            jax.ShapeDtypeStruct((rows, width), f32),
            jax.ShapeDtypeStruct((2 * rows, width), jnp.bfloat16),
            jax.ShapeDtypeStruct((every, rows, width), jnp.bfloat16),
            jax.ShapeDtypeStruct((width, every * width), f32),
            jax.ShapeDtypeStruct((width, every * width), f32),
        ],
        in_specs=[smem, smem, vmem, pl.BlockSpec(memory_space=pl.ANY)],
        out_specs=[vmem] * 6,
        scratch_shapes=[
            pltpu.VMEM(tiles.shape, tiles.dtype),
            pltpu.VMEM((3, rows + 16 * T, width), jnp.bfloat16),
            pltpu.VMEM((rows, width), f32),
            pltpu.VMEM((rows, width), f32),
            pltpu.VMEM((every, rows, width), jnp.bfloat16),
            pltpu.VMEM((4 * T, rows), jnp.bfloat16),
            sems(()),
            sems((3, 2)), sems((3, 2)), sems((2, 6)), sems((2, 6)), sems((2, 4)), sems((2, 4)),
        ],
        compiler_params=pltpu.CompilerParams(collective_id=0, has_side_effects=True, vmem_limit_bytes=48 << 20),
    )(slots, weights, seed, tiles)


def by_offset(tile_cols, tile_count, tile_scale):
    local_blocks, slot_total = tile_cols.shape
    reach = (slot_total - 1) // 2
    total = local_blocks * lax.axis_size("node")
    row = jnp.arange(local_blocks)[:, None]
    where = jnp.mod(tile_cols - (lax.axis_index("node") * local_blocks + row) + reach, total)
    slot = jnp.arange(slot_total)[None, :]
    weights = jnp.where(slot < tile_count[:, None], tile_scale, 0.0)
    hit = where[:, :, None] == jnp.arange(slot_total)[None, None, :]
    slots = jnp.sum(jnp.where(hit, (row * slot_total + slot)[:, :, None], 0), axis=1)
    return slots.reshape(-1), jnp.sum(jnp.where(hit, weights[:, :, None], 0.0), axis=1).reshape(-1)


def sum_kernel(ct_ref, xt_ref, parts_ref, full_ref, xs_ref, image_ref,
               first_ref, part_ref, second_ref,
               send1, recv1, send2, recv2, send_a, recv_a, send_b, recv_b, send_c, recv_c,
               send_t, recv_t, send_xb, recv_xb, send_xc, recv_xc, ring_send, ring_recv, pair_send, pair_recv):
    side = 4
    node, cls = lax.axis_index("node"), lax.axis_index("cls")
    chip, core = cls // 2, cls % 2
    y, z = node // side, node % side
    f = jnp.where(core == 0, z, y)
    s = jnp.where(core == 0, y, z)
    rows = parts_ref.shape[0] // 2
    half = rows // 2

    def at(f_, s_):
        return {"node": jnp.where(core == 0, s_ * side + f_, f_ * side + s_)}

    def turn(v, m):
        return (v + m) % side

    along_f = [at(turn(f, m), s) for m in range(1, side)]
    along_s = [at(f, turn(s, m)) for m in range(1, side)]
    along_x = [{"cls": turn(chip, m) * 2 + core} for m in range(1, side)]
    twin = {"cls": chip * 2 + 1 - core}
    greet(along_f + along_s + along_x + [twin])

    pending = []

    def go(copies):
        for copy in copies:
            copy.start()
        pending.extend(copies)
        return copies

    grams = (ct_ref, xt_ref)

    def stage1(q):
        return go([remote(grams[q].at[:, turn(f, m)], first_ref.at[q, m - 1],
                          send1.at[q, m - 1], recv1.at[q, m - 1], along_f[m - 1])
                   for m in range(1, side)])

    def stage2(q, before):
        for copy in before:
            copy.wait_recv()
        for k in range(side):
            part_ref[q, k] = (grams[q][k, f] + first_ref[q, 0, k]) + (first_ref[q, 1, k] + first_ref[q, 2, k])
        return go([remote(part_ref.at[q, turn(s, m)], second_ref.at[q, m - 1],
                          send2.at[q, m - 1], recv2.at[q, m - 1], along_s[m - 1])
                   for m in range(1, side)])

    def finish(q, before):
        for copy in before:
            copy.wait_recv()
        return (part_ref[q, s] + second_ref[q, 0]) + (second_ref[q, 1] + second_ref[q, 2])

    before, after, across = turn(chip, 3), turn(chip, 1), turn(chip, 2)
    to_right, to_left = along_x[0], along_x[2]

    def ring_copy(q, n, owner, part, to):
        ref = image_ref.at[q, owner, pl.ds(part * half, half)]
        return remote(ref, ref, ring_send.at[q, n], ring_recv.at[q, n], to)

    def pair_copy(q, n, owner):
        ref = image_ref.at[q, owner]
        return remote(ref, ref, pair_send.at[q, n], pair_recv.at[q, n], twin)

    def image_first(q):
        return go([ring_copy(q, 0, cls, 0, to_right), ring_copy(q, 1, cls, 1, to_left),
                   ring_copy(q, 2, cls, 1, to_right), ring_copy(q, 3, cls, 0, to_left)])

    def image_second(q, sent):
        sent[0].wait_recv()
        a = go([ring_copy(q, 4, before * 2 + core, 0, to_right)])
        sent[1].wait_recv()
        b = go([ring_copy(q, 5, after * 2 + core, 1, to_left)])
        sent[2].wait_recv()
        c = go([pair_copy(q, 1, before * 2 + core)])
        sent[3].wait_recv()
        d = go([pair_copy(q, 2, after * 2 + core)])
        return a + b, c + d

    def image_last(q, sent):
        for copy in sent:
            copy.wait_recv()
        return go([pair_copy(q, 3, across * 2 + core)])

    c1 = stage1(0)
    image_ref[0, cls] = parts_ref[0:rows, :]
    image_ref[1, cls] = parts_ref[rows:, :]
    top1 = image_first(0)
    c2 = stage2(0, c1)
    x1 = stage1(1)
    full_ref[chip, core, s, f] = finish(0, c2)
    mine = full_ref.at[chip, core, s, f]
    stage_a = go([remote(mine, mine, send_a.at[m], recv_a.at[m], along_x[m]) for m in range(side - 1)])
    x2 = stage2(1, x1)
    for copy in stage_a:
        copy.wait_recv()
    line = full_ref.at[:, core, s, f]
    stage_b = go([remote(line, line, send_b.at[m], recv_b.at[m], along_f[m]) for m in range(side - 1)])
    low1 = image_first(1)
    shared_image = go([pair_copy(q, 0, cls) for q in range(2)])
    xs_ref[s, f] = finish(1, x2)
    mine_x = xs_ref.at[s, f]
    stage_xb = go([remote(mine_x, mine_x, send_xb.at[m], recv_xb.at[m], along_f[m]) for m in range(side - 1)])
    top2, more = image_second(0, top1)
    shared_image += more
    for copy in stage_b:
        copy.wait_recv()

    def slab(owner, h):
        return full_ref.at[pl.ds(2 * h, 2), core, owner]

    def ring(n, owner, h, to):
        return remote(slab(owner, h), slab(owner, h), send_c.at[n], recv_c.at[n], to)

    def share(n, owner, h):
        return remote(slab(owner, h), slab(owner, h), send_t.at[n], recv_t.at[n], twin)

    up, down = along_s[0], along_s[2]
    below, above, far = turn(s, 3), turn(s, 1), turn(s, 2)
    r0, r1, r2, r3 = go([ring(0, s, 0, up), ring(1, s, 1, down), ring(2, s, 1, up), ring(3, s, 0, down)])
    shared = go([share(0, s, 0), share(1, s, 1)])
    for copy in stage_xb:
        copy.wait_recv()
    line_x = xs_ref.at[s]
    stage_xc = go([remote(line_x, line_x, send_xc.at[m], recv_xc.at[m], along_s[m]) for m in range(side - 1)])
    r0.wait_recv()
    fwd0, = go([ring(4, below, 0, up)])
    r1.wait_recv()
    fwd1, = go([ring(5, above, 1, down)])
    shared += go([share(2, below, 0), share(3, above, 1)])
    shared_image += image_last(0, top2)
    r2.wait_recv()
    shared += go([share(4, below, 1)])
    r3.wait_recv()
    shared += go([share(5, above, 0)])
    low2, more = image_second(1, low1)
    shared_image += more
    fwd0.wait_recv()
    shared += go([share(6, far, 0)])
    fwd1.wait_recv()
    shared += go([share(7, far, 1)])
    shared_image += image_last(1, low2)
    for copy in stage_xc + shared + shared_image:
        copy.wait_recv()
    for copy in pending:
        copy.wait_send()


def sum_and_share(ct, xt, parts):
    width, classes = ct.shape
    f32 = jnp.float32
    vmem = pl.BlockSpec(memory_space=pltpu.VMEM)
    sems = pltpu.SemaphoreType.DMA
    cut = (4, 4, width // 16, classes)
    rows = parts.shape[0] // 2
    full, xs, image = pl.pallas_call(
        sum_kernel,
        out_shape=[jax.ShapeDtypeStruct((4, 2) + cut, f32), jax.ShapeDtypeStruct(cut, f32),
                   jax.ShapeDtypeStruct((2, classes // width, rows, width), parts.dtype)],
        in_specs=[vmem] * 3,
        out_specs=[vmem] * 3,
        scratch_shapes=[
            pltpu.VMEM((2, 3, 4, width // 16, classes), f32),
            pltpu.VMEM((2, 4, width // 16, classes), f32),
            pltpu.VMEM((2, 3, width // 16, classes), f32),
            sems((2, 3)), sems((2, 3)), sems((2, 3)), sems((2, 3)),
            sems((3,)), sems((3,)), sems((3,)), sems((3,)), sems((6,)), sems((6,)),
            sems((8,)), sems((8,)), sems((3,)), sems((3,)), sems((3,)), sems((3,)),
            sems((2, 6)), sems((2, 6)), sems((2, 4)), sems((2, 4)),
        ],
        compiler_params=pltpu.CompilerParams(collective_id=1, has_side_effects=True, vmem_limit_bytes=32 << 20),
    )(ct.reshape(cut), xt.reshape(cut), parts)
    return full.reshape(classes, classes), xs.reshape(width, classes), image


ND = 2

def dot(a, b, dims=((1,), (0,))):
    return lax.dot_general(a, b, (dims, ((), ())), precision=HI, preferred_element_type=jnp.float32)

def row_of(x, j):
    return jnp.broadcast_to(x[j:j + 1, :], (8, T))

def factor(rows):
    lane = lax.broadcasted_iota(jnp.int32, (8, T), 1)
    sub = lax.broadcasted_iota(jnp.int32, (8, T), 0)
    own = [sub == j for j in range(8)]
    out = []

    def splat(x, c):
        return jnp.broadcast_to(x[:, c:c + 1], (8, T))

    ahead = [splat(rows[0], c) for c in range(8)]
    for k in range(16):
        last = k == 15
        inside = (lane >= 8 * k) & (lane < 8 * k + 8)
        b = ahead
        later = [] if last else [splat(rows[k], 8 * k + 8 + c) for c in range(8)]
        cols = [[splat(r, 8 * k + j) for j in range(8)] for r in rows[k + 1:k + 1 + ND]]
        fresh = [] if last else [splat(rows[k + 1], 8 * k + 8 + c) for c in range(8)]
        panel = jnp.where(inside, jnp.where(lane - 8 * k == sub, 1.0, 0.0), rows[k])
        done = jnp.zeros((8, T), jnp.float32)
        for j in range(8):
            p = row_of(b[j], j)
            r = 1.0 / p
            f = b[j]

            def clear(x):
                n = row_of(x, j) * r
                return jnp.where(own[j], n, x - f * n)

            done = jnp.where(own[j], row_of(panel, j) * lax.rsqrt(p), done)
            for l in range(j + 1, 8):
                b[l] = clear(b[l])
            later = [clear(x) for x in later]
            panel = clear(panel)
        out.append(jnp.where(lane < 8 * k + 8, done, 0.0))
        if last:
            break
        ahead = []
        for c in range(8):
            terms = [cols[0][j] * row_of(later[c], j) for j in range(8)]
            while len(terms) > 1:
                terms = [terms[i] + terms[i + 1] for i in range(0, len(terms), 2)]
            ahead.append(fresh[c] - terms[0])
        spread = [row_of(panel, j) for j in range(8)]
        near = min(k + 1 + ND, 16)
        if near < 16:
            wide = [jnp.zeros((8, T), jnp.float32)] * 16
            wide[k] = panel
            away = dot(jnp.concatenate(rows[near:], axis=0), jnp.concatenate(wide, axis=0))
        for g in range(k + 1, 16):
            acc = jnp.where(inside, 0.0, rows[g])
            if g < near:
                for j in range(8):
                    acc = acc - cols[g - k - 1][j] * spread[j]
            else:
                acc = acc - away[8 * (g - near):8 * (g - near) + 8]
            rows[g] = acc
    return out

def solve_kernel(c_ref, x_ref, d_hbm, r_hbm, high_hbm, image_hbm, out_d_ref, out_r_ref,
                 a_ref, l_ref, v_ref, z_ref, d_ref, r_ref, high_ref, image_ref, sem):
    fetches = [pltpu.make_async_copy(a, b, sem.at[i]) for i, (a, b) in enumerate((
        (d_hbm, d_ref), (r_hbm, r_ref), (high_hbm, high_ref), (image_hbm, image_ref)))]
    for fetch in fetches:
        fetch.start()
    n = c_ref.shape[0]
    nb = n // T
    wide = n + T
    for i in range(nb):
        for j in range(i, nb):
            a_ref[i * T:(i + 1) * T, j * T:(j + 1) * T] = 0.5 * (
                c_ref[i * T:(i + 1) * T, j * T:(j + 1) * T] + c_ref[j * T:(j + 1) * T, i * T:(i + 1) * T].T)
    start = pl.multiple_of(lax.axis_index("cls") * T, T)
    for i in range(nb):
        here = slice(i * T, (i + 1) * T)
        a_ref[here, n:] = (x_ref[:, here] + 0.5 * c_ref[pl.ds(start, T), here]).T - 0.5 * c_ref[here, pl.ds(start, T)]
    def update(k, i):
        here, there = slice(k * T, (k + 1) * T), slice(i * T, (i + 1) * T)
        a_ref[there, i * T:] -= dot(v_ref[here, there], v_ref[here, i * T:], ((0,), (0,)))

    for k in range(nb):
        here = slice(k * T, (k + 1) * T)
        rows = factor([a_ref[k * T + 8 * g:k * T + 8 * g + 8, here] for g in range(16)])
        for i in range(k + 1, nb):
            if k:
                update(k - 1, i)
        for g in range(16):
            l_ref[k * T + 8 * g:k * T + 8 * g + 8, :] = rows[g]
        v_ref[here, (k + 1) * T:] = dot(l_ref[here, :], a_ref[here, (k + 1) * T:])
        if k + 1 < nb:
            update(k, k + 1)
    y = v_ref[:, n:]
    for j in range(nb - 1, -1, -1):
        here = slice(j * T, (j + 1) * T)
        known = dot(l_ref[here, :], y[here], ((0,), (0,)))
        z_ref[here, :] = known
        if j:
            y = y[:j * T] - dot(v_ref[:j * T, here], known)
    for fetch in fetches:
        fetch.wait()
    every = high_ref.shape[0]

    def products(t, _):
        at = pl.ds(pl.multiple_of(t * 2 * T, 2 * T), 2 * T)
        mixed = d_ref[at, :]
        left = r_ref[at, :]
        for m in range(every // 2):
            z = z_ref[m * 2 * T:(m + 1) * 2 * T, :]
            top = z.astype(jnp.bfloat16)
            rest = (z - top.astype(jnp.float32)).astype(jnp.bfloat16)
            both = jnp.concatenate([top, rest], axis=1)
            high = jnp.concatenate([high_ref[2 * m, at, :], high_ref[2 * m + 1, at, :]], axis=1)
            coarse = jnp.concatenate([image_ref[0, 2 * m, at, :], image_ref[0, 2 * m + 1, at, :]], axis=1)
            fine = jnp.concatenate([image_ref[1, 2 * m, at, :], image_ref[1, 2 * m + 1, at, :]], axis=1)
            mixed += jnp.dot(high, top, preferred_element_type=jnp.float32)
            pair = jnp.dot(coarse, both, preferred_element_type=jnp.float32)
            left -= pair[:, :T] + (pair[:, T:] + jnp.dot(fine, top, preferred_element_type=jnp.float32))
        out_d_ref[at, :] = mixed
        out_r_ref[at, :] = left
        return 0

    lax.fori_loop(0, d_ref.shape[0] // (2 * T), products, 0)


def solve(c, x, direction, misfit, high, image):
    n = c.shape[0]
    rows = direction.shape[0]
    f32 = jnp.float32
    vmem, hbm = pl.BlockSpec(memory_space=pltpu.VMEM), pl.BlockSpec(memory_space=pl.ANY)
    return pl.pallas_call(
        solve_kernel,
        out_shape=[jax.ShapeDtypeStruct((rows, T), f32)] * 2,
        in_specs=[vmem] * 2 + [hbm] * 4,
        out_specs=[vmem] * 2,
        scratch_shapes=[pltpu.VMEM((n, n + T), f32), pltpu.VMEM((n, T), f32), pltpu.VMEM((n, n + T), f32),
                        pltpu.VMEM((n, T), f32), pltpu.VMEM((rows, T), f32), pltpu.VMEM((rows, T), f32),
                        pltpu.VMEM(high.shape, high.dtype), pltpu.VMEM(image.shape, image.dtype),
                        pltpu.SemaphoreType.DMA((4,))],
        compiler_params=pltpu.CompilerParams(vmem_limit_bytes=48 << 20),
    )(c, x, direction, misfit, high, image)


def body(seed_scores, tile_vals, tile_cols, tile_count, tile_scale):
    slots, weights = by_offset(tile_cols, tile_count, tile_scale)
    tiles = tile_vals.reshape(-1, T, T)
    direction, misfit, parts, high, ct, xt = find_direction(slots, weights, seed_scores, tiles)
    full, xs, image = sum_and_share(ct, xt, parts)
    return tuple(solve(full, xs, direction, misfit, high, image))


def solution(mesh):
    return jax.shard_map(
        body,
        mesh=mesh,
        in_specs=(
            P("node", "cls"),
            P("node", None, None, None),
            P("node", None),
            P("node"),
            P("node", None),
        ),
        out_specs=(P("node", "cls"), P("node", "cls")),
        check_vma=False,
    )
```

```python
import functools
import jax
import jax.numpy as jnp
from jax import lax
from jax.experimental import pallas as pl
from jax.experimental.pallas import tpu as pltpu
from jax.sharding import PartitionSpec as P

SHRINK = 0.9
HI = lax.Precision.HIGHEST
MESH = pl.DeviceIdType.MESH
T = 128
GUESS = (-2.9, 2.34)


def remote(src, dst, send, recv, to):
    return pltpu.make_async_remote_copy(
        src_ref=src, dst_ref=dst, send_sem=send, recv_sem=recv, device_id=to, device_id_type=MESH)


def greet(peers):
    barrier = pltpu.get_barrier_semaphore()
    for peer in peers:
        pl.semaphore_signal(barrier, inc=1, device_id=peer, device_id_type=MESH)
    pl.semaphore_wait(barrier, len(peers))


def direction_kernel(slot_ref, weight_ref, seed_ref, tiles_hbm,
                     d_ref, r_ref, parts_ref, spread_hbm, ct_ref, xt_ref,
                     tiles_ref, ext_ref, acc_ref, z_ref, all_ref, flat_ref, sum_ref, tiles_sem, out_sem,
                     halo_send, halo_recv, ring_send, ring_recv, pair_send, pair_recv):
    fetch = pltpu.make_async_copy(tiles_hbm, tiles_ref, tiles_sem)
    fetch.start()
    blocks = acc_ref.shape[0] // T
    reach = 8
    rows = blocks * T
    half = rows // 2
    edge = reach * T
    node, cls = lax.axis_index("node"), lax.axis_index("cls")
    nodes = lax.axis_size("node")
    chips = lax.axis_size("cls") // 2
    chip, core = cls // 2, cls % 2
    right_node, left_node = {"node": (node + 1) % nodes}, {"node": (node + nodes - 1) % nodes}
    right_chip, left_chip, far_chip = (chip + 1) % chips, (chip + chips - 1) % chips, (chip + 2) % chips
    right, left, twin = {"cls": right_chip * 2 + core}, {"cls": left_chip * 2 + core}, {"cls": chip * 2 + 1 - core}
    greet([right_node, left_node, right, left, twin])

    def halo_copies(s):
        ext = ext_ref.at[s]
        return (
            remote(ext.at[pl.ds(rows, edge)], ext.at[pl.ds(0, edge)],
                   halo_send.at[s, 0], halo_recv.at[s, 0], right_node),
            remote(ext.at[pl.ds(edge, edge)], ext.at[pl.ds(edge + rows, edge)],
                   halo_send.at[s, 1], halo_recv.at[s, 1], left_node),
        )

    def product(s, tile, source):
        return jnp.dot(tiles_ref[tile], ext_ref[s, pl.ds(pl.multiple_of(source * T, T), T), :],
                       preferred_element_type=jnp.float32)

    def spread(s, z):
        ext_ref[s, edge:edge + rows, :] = z.astype(jnp.bfloat16)
        copies = halo_copies(s)
        for copy in copies:
            copy.start()
        return copies

    def local_part(s):
        def one(i, _):
            total = jnp.zeros((T, T), jnp.float32)
            for j in range(blocks):
                o = j + reach - i
                fits = (o >= 0) & (o <= 2 * reach)
                at = i * (2 * reach + 1) + jnp.clip(o, 0, 2 * reach)
                w = jnp.where(fits, weight_ref[at], 0.0)
                total += w * product(s, slot_ref[at], j + reach)
            acc_ref[pl.ds(pl.multiple_of(i * T, T), T), :] = total
            return 0
        lax.fori_loop(0, blocks, one, 0)

    def edge_part(s):
        def one(t, _):
            low = jnp.zeros((T, T), jnp.float32)
            high = jnp.zeros((T, T), jnp.float32)
            for m in range(reach + 1):
                lower = m < reach - t
                i = jnp.where(lower, t, t + blocks - reach)
                j = t + m + jnp.where(lower, 0, blocks)
                at = i * (2 * reach + 1) + j - i
                w = weight_ref[at]
                p = product(s, slot_ref[at], j)
                low += jnp.where(lower, w, 0.0) * p
                high += jnp.where(lower, 0.0, w) * p
            acc_ref[pl.ds(pl.multiple_of(t * T, T), T), :] += low
            acc_ref[pl.ds(pl.multiple_of((t + blocks - reach) * T, T), T), :] += high
            return 0
        lax.fori_loop(0, reach, one, 0)

    def operate(s, copies):
        local_part(s)
        for copy in copies:
            copy.wait_recv()
        edge_part(s)

    def ring_copy(q, n, owner, part, to):
        ref = all_ref.at[q, owner, pl.ds(part * half, half)]
        return remote(ref, ref, ring_send.at[q, n], ring_recv.at[q, n], to)

    def twin_copy(q, n, owner):
        ref = all_ref.at[q, owner]
        return remote(ref, ref, pair_send.at[q, n], pair_recv.at[q, n], twin)

    pending = []

    def go(copies):
        for copy in copies:
            copy.start()
        pending.extend(copies)
        return copies

    def ring_first(q, value):
        all_ref[q, cls] = value.astype(jnp.bfloat16)
        return go([ring_copy(q, 0, cls, 0, right), ring_copy(q, 1, cls, 1, left),
                   ring_copy(q, 2, cls, 1, right), ring_copy(q, 3, cls, 0, left)]), go([twin_copy(q, 0, cls)])

    def ring_second(q, sent):
        sent[0].wait_recv()
        a = go([ring_copy(q, 4, left_chip * 2 + core, 0, right)])
        sent[1].wait_recv()
        b = go([ring_copy(q, 5, right_chip * 2 + core, 1, left)])
        sent[2].wait_recv()
        c = go([twin_copy(q, 1, left_chip * 2 + core)])
        sent[3].wait_recv()
        d = go([twin_copy(q, 2, right_chip * 2 + core)])
        return a + b, c, d

    def ring_last(q, sent):
        for copy in sent:
            copy.wait_recv()
        return go([twin_copy(q, 3, far_chip * 2 + core)])

    def grams(q, which):
        both = jnp.concatenate([all_ref[q, which * 2], all_ref[q, which * 2 + 1]], axis=1)
        at = pl.ds(pl.multiple_of(which * 2 * T, 2 * T), 2 * T)
        out = jnp.dot(flat_ref[...], both, preferred_element_type=jnp.float32)
        image_part, r_part = out[0:T] + out[2 * T:3 * T], out[T:2 * T] + out[3 * T:]
        if q == 0:
            ct_ref[:, at] = image_part
            xt_ref[:, at] = r_part
        else:
            ct_ref[:, at] += image_part
            xt_ref[:, at] += r_part

    def keep(m):
        def one(t, _):
            at = pl.ds(pl.multiple_of(t * T, T), T)
            for n in range(2):
                total = all_ref[0, 2 * m + n, at, :].astype(jnp.float32) + all_ref[1, 2 * m + n, at, :].astype(jnp.float32)
                total = total + all_ref[2, 2 * m + n, at, :].astype(jnp.float32)
                sum_ref[2 * m + n, at, :] = total.astype(jnp.bfloat16)
            return 0
        lax.fori_loop(0, blocks, one, 0)
        at = pl.ds(2 * m, 2)
        return pltpu.make_async_copy(sum_ref.at[at], spread_hbm.at[at], out_sem.at[m])

    factor = SHRINK
    z_ref[...] = seed_ref[...]
    d_ref[...] = seed_ref[...]
    firsts, owns, seconds = [], [], []
    for s in range(2):
        copies = spread(s, z_ref[...])
        pending.extend(copies)
        if s:
            seconds.append(ring_second(0, firsts[0]))
        first, own = ring_first(s, GUESS[s] * z_ref[...])
        firsts.append(first)
        owns.append(own)
        if s == 0:
            fetch.wait()
        operate(s, copies)
        factor_next = 1.0 / (2.0 / SHRINK - factor)
        misfit = seed_ref[...] - (z_ref[...] - SHRINK * acc_ref[...])
        update = factor_next * factor * d_ref[...] + (2.0 * factor_next / SHRINK) * misfit
        d_ref[...] = update
        z_ref[...] = z_ref[...] + update
        factor = factor_next
    z = z_ref[...]
    d_ref[...] = z
    copies = spread(2, z)
    pending.extend(copies)
    seconds.append(ring_second(1, firsts[1]))
    first, own = ring_first(2, z - all_ref[0, cls].astype(jnp.float32) - all_ref[1, cls].astype(jnp.float32))
    lasts = [ring_last(0, seconds[0][0])]
    operate(2, copies)
    second = ring_second(2, first)
    image = z_ref[...] - SHRINK * acc_ref[...]
    r_ref[...] = seed_ref[...] - image
    coarse = image.astype(jnp.bfloat16)
    parts_ref[0:rows, :] = coarse
    parts_ref[rows:, :] = (image - coarse.astype(jnp.float32)).astype(jnp.bfloat16)
    lasts.append(ring_last(1, seconds[1][0]))

    image_t = image.T
    r_t = r_ref[...].T
    for n, value in enumerate((image_t, r_t)):
        top = value.astype(jnp.bfloat16)
        flat_ref[n * T:(n + 1) * T, :] = top
        flat_ref[(2 + n) * T:(3 + n) * T, :] = (value - top.astype(jnp.float32)).astype(jnp.bfloat16)

    for q in range(2):
        for copy in owns[q] + list(seconds[q][1]) + list(seconds[q][2]) + lasts[q]:
            copy.wait_recv()
        for m in range(chips):
            grams(q, m)
    kept = []

    def third(m):
        grams(2, m)
        kept.append(keep(m))
        kept[-1].start()

    own[0].wait_recv()
    third(chip)
    last = ring_last(2, second[0])
    second[1][0].wait_recv()
    third(left_chip)
    second[2][0].wait_recv()
    third(right_chip)
    last[0].wait_recv()
    third(far_chip)
    for copy in pending:
        copy.wait_send()
    for copy in kept:
        copy.wait()


def find_direction(slots, weights, seed, tiles):
    rows, width = seed.shape
    every = lax.axis_size("cls")
    f32 = jnp.float32
    vmem = pl.BlockSpec(memory_space=pltpu.VMEM)
    smem = pl.BlockSpec(memory_space=pltpu.SMEM)
    hbm = pl.BlockSpec(memory_space=pl.ANY)
    sems = pltpu.SemaphoreType.DMA
    return pl.pallas_call(
        direction_kernel,
        out_shape=[
            jax.ShapeDtypeStruct((rows, width), f32),
            jax.ShapeDtypeStruct((rows, width), f32),
            jax.ShapeDtypeStruct((2 * rows, width), jnp.bfloat16),
            jax.ShapeDtypeStruct((every, rows, width), jnp.bfloat16),
            jax.ShapeDtypeStruct((width, every * width), f32),
            jax.ShapeDtypeStruct((width, every * width), f32),
        ],
        in_specs=[smem, smem, vmem, hbm],
        out_specs=[vmem] * 3 + [hbm] + [vmem] * 2,
        scratch_shapes=[
            pltpu.VMEM(tiles.shape, tiles.dtype),
            pltpu.VMEM((3, rows + 16 * T, width), jnp.bfloat16),
            pltpu.VMEM((rows, width), f32),
            pltpu.VMEM((rows, width), f32),
            pltpu.VMEM((3, every, rows, width), jnp.bfloat16),
            pltpu.VMEM((4 * T, rows), jnp.bfloat16),
            pltpu.VMEM((every, rows, width), jnp.bfloat16),
            sems(()), sems((4,)),
            sems((3, 2)), sems((3, 2)), sems((3, 6)), sems((3, 6)), sems((3, 4)), sems((3, 4)),
        ],
        compiler_params=pltpu.CompilerParams(collective_id=0, has_side_effects=True, vmem_limit_bytes=48 << 20),
    )(slots, weights, seed, tiles)


def by_offset(tile_cols, tile_count, tile_scale):
    local_blocks, slot_total = tile_cols.shape
    reach = (slot_total - 1) // 2
    total = local_blocks * lax.axis_size("node")
    row = jnp.arange(local_blocks)[:, None]
    where = jnp.mod(tile_cols - (lax.axis_index("node") * local_blocks + row) + reach, total)
    slot = jnp.arange(slot_total)[None, :]
    weights = jnp.where(slot < tile_count[:, None], tile_scale, 0.0)
    hit = where[:, :, None] == jnp.arange(slot_total)[None, None, :]
    slots = jnp.sum(jnp.where(hit, (row * slot_total + slot)[:, :, None], 0), axis=1)
    return slots.reshape(-1), jnp.sum(jnp.where(hit, weights[:, :, None], 0.0), axis=1).reshape(-1)


def sum_kernel(ct_ref, xt_ref, parts_ref, full_ref, xs_ref, image_ref,
               first_ref, part_ref, second_ref,
               send1, recv1, send2, recv2, send_a, recv_a, send_b, recv_b, send_c, recv_c,
               send_t, recv_t, send_xb, recv_xb, send_xc, recv_xc, ring_send, ring_recv, pair_send, pair_recv, place_sem):
    side = 4
    node, cls = lax.axis_index("node"), lax.axis_index("cls")
    chip, core = cls // 2, cls % 2
    y, z = node // side, node % side
    f = jnp.where(core == 0, z, y)
    s = jnp.where(core == 0, y, z)
    rows = parts_ref.shape[0] // 2
    half = rows // 2

    def at(f_, s_):
        return {"node": jnp.where(core == 0, s_ * side + f_, f_ * side + s_)}

    def turn(v, m):
        return (v + m) % side

    along_f = [at(turn(f, m), s) for m in range(1, side)]
    along_s = [at(f, turn(s, m)) for m in range(1, side)]
    along_x = [{"cls": turn(chip, m) * 2 + core} for m in range(1, side)]
    twin = {"cls": chip * 2 + 1 - core}
    greet(along_f + along_s + along_x + [twin])

    pending = []

    def go(copies):
        for copy in copies:
            copy.start()
        pending.extend(copies)
        return copies

    grams = (ct_ref, xt_ref)

    def stage1(q):
        return go([remote(grams[q].at[:, turn(f, m)], first_ref.at[q, m - 1],
                          send1.at[q, m - 1], recv1.at[q, m - 1], along_f[m - 1])
                   for m in range(1, side)])

    def stage2(q, before):
        for copy in before:
            copy.wait_recv()
        for k in range(side):
            part_ref[q, k] = (grams[q][k, f] + first_ref[q, 0, k]) + (first_ref[q, 1, k] + first_ref[q, 2, k])
        return go([remote(part_ref.at[q, turn(s, m)], second_ref.at[q, m - 1],
                          send2.at[q, m - 1], recv2.at[q, m - 1], along_s[m - 1])
                   for m in range(1, side)])

    def finish(q, before):
        for copy in before:
            copy.wait_recv()
        return (part_ref[q, s] + second_ref[q, 0]) + (second_ref[q, 1] + second_ref[q, 2])

    before, after, across = turn(chip, 3), turn(chip, 1), turn(chip, 2)
    to_right, to_left = along_x[0], along_x[2]

    def ring_copy(q, n, owner, part, to):
        ref = image_ref.at[q, owner, pl.ds(part * half, half)]
        return remote(ref, ref, ring_send.at[q, n], ring_recv.at[q, n], to)

    def pair_copy(q, n, owner):
        ref = image_ref.at[q, owner]
        return remote(ref, ref, pair_send.at[q, n], pair_recv.at[q, n], twin)

    def image_first(q):
        return go([ring_copy(q, 0, cls, 0, to_right), ring_copy(q, 1, cls, 1, to_left),
                   ring_copy(q, 2, cls, 1, to_right), ring_copy(q, 3, cls, 0, to_left)])

    def image_second(q, sent):
        sent[0].wait_recv()
        a = go([ring_copy(q, 4, before * 2 + core, 0, to_right)])
        sent[1].wait_recv()
        b = go([ring_copy(q, 5, after * 2 + core, 1, to_left)])
        sent[2].wait_recv()
        c = go([pair_copy(q, 1, before * 2 + core)])
        sent[3].wait_recv()
        d = go([pair_copy(q, 2, after * 2 + core)])
        return a + b, c + d

    def image_last(q, sent):
        for copy in sent:
            copy.wait_recv()
        return go([pair_copy(q, 3, across * 2 + core)])

    c1 = stage1(0)
    place = [pltpu.make_async_copy(parts_ref.at[pl.ds(q * rows, rows)], image_ref.at[q, cls], place_sem.at[q]) for q in range(2)]
    for copy in place:
        copy.start()
    for copy in place:
        copy.wait()
    top1 = image_first(0)
    c2 = stage2(0, c1)
    x1 = stage1(1)
    full_ref[chip, core, s, f] = finish(0, c2)
    mine = full_ref.at[chip, core, s, f]
    stage_a = go([remote(mine, mine, send_a.at[m], recv_a.at[m], along_x[m]) for m in range(side - 1)])
    x2 = stage2(1, x1)
    for copy in stage_a:
        copy.wait_recv()
    line = full_ref.at[:, core, s, f]
    stage_b = go([remote(line, line, send_b.at[m], recv_b.at[m], along_f[m]) for m in range(side - 1)])
    low1 = image_first(1)
    shared_image = go([pair_copy(q, 0, cls) for q in range(2)])
    xs_ref[s, f] = finish(1, x2)
    mine_x = xs_ref.at[s, f]
    stage_xb = go([remote(mine_x, mine_x, send_xb.at[m], recv_xb.at[m], along_f[m]) for m in range(side - 1)])
    top2, more = image_second(0, top1)
    shared_image += more
    for copy in stage_b:
        copy.wait_recv()

    def slab(owner, h):
        return full_ref.at[pl.ds(2 * h, 2), core, owner]

    def ring(n, owner, h, to):
        return remote(slab(owner, h), slab(owner, h), send_c.at[n], recv_c.at[n], to)

    def share(n, owner, h):
        return remote(slab(owner, h), slab(owner, h), send_t.at[n], recv_t.at[n], twin)

    up, down = along_s[0], along_s[2]
    below, above, far = turn(s, 3), turn(s, 1), turn(s, 2)
    r0, r1, r2, r3 = go([ring(0, s, 0, up), ring(1, s, 1, down), ring(2, s, 1, up), ring(3, s, 0, down)])
    shared = go([share(0, s, 0), share(1, s, 1)])
    for copy in stage_xb:
        copy.wait_recv()
    line_x = xs_ref.at[s]
    stage_xc = go([remote(line_x, line_x, send_xc.at[m], recv_xc.at[m], along_s[m]) for m in range(side - 1)])
    r0.wait_recv()
    fwd0, = go([ring(4, below, 0, up)])
    r1.wait_recv()
    fwd1, = go([ring(5, above, 1, down)])
    shared += go([share(2, below, 0), share(3, above, 1)])
    shared_image += image_last(0, top2)
    r2.wait_recv()
    shared += go([share(4, below, 1)])
    r3.wait_recv()
    shared += go([share(5, above, 0)])
    low2, more = image_second(1, low1)
    shared_image += more
    fwd0.wait_recv()
    shared += go([share(6, far, 0)])
    fwd1.wait_recv()
    shared += go([share(7, far, 1)])
    shared_image += image_last(1, low2)
    for copy in stage_xc + shared + shared_image:
        copy.wait_recv()
    for copy in pending:
        copy.wait_send()


def sum_and_share(ct, xt, parts):
    width, classes = ct.shape
    f32 = jnp.float32
    vmem = pl.BlockSpec(memory_space=pltpu.VMEM)
    sems = pltpu.SemaphoreType.DMA
    cut = (4, 4, width // 16, classes)
    hbm = pl.BlockSpec(memory_space=pl.ANY)
    rows = parts.shape[0] // 2
    full, xs, image = pl.pallas_call(
        sum_kernel,
        out_shape=[jax.ShapeDtypeStruct((4, 2) + cut, f32), jax.ShapeDtypeStruct(cut, f32),
                   jax.ShapeDtypeStruct((2, classes // width, rows, width), parts.dtype)],
        in_specs=[vmem, vmem, hbm],
        out_specs=[vmem, vmem, hbm],
        scratch_shapes=[
            pltpu.VMEM((2, 3, 4, width // 16, classes), f32),
            pltpu.VMEM((2, 4, width // 16, classes), f32),
            pltpu.VMEM((2, 3, width // 16, classes), f32),
            sems((2, 3)), sems((2, 3)), sems((2, 3)), sems((2, 3)),
            sems((3,)), sems((3,)), sems((3,)), sems((3,)), sems((6,)), sems((6,)),
            sems((8,)), sems((8,)), sems((3,)), sems((3,)), sems((3,)), sems((3,)),
            sems((2, 6)), sems((2, 6)), sems((2, 4)), sems((2, 4)), sems((2,)),
        ],
        compiler_params=pltpu.CompilerParams(collective_id=1, has_side_effects=True, vmem_limit_bytes=32 << 20),
    )(ct.reshape(cut), xt.reshape(cut), parts)
    return full.reshape(classes, classes), xs.reshape(width, classes), image


ND = 2

def dot(a, b, dims=((1,), (0,))):
    return lax.dot_general(a, b, (dims, ((), ())), precision=HI, preferred_element_type=jnp.float32)

def row_of(x, j):
    return jnp.broadcast_to(x[j:j + 1, :], (8, T))

def factor(rows):
    lane = lax.broadcasted_iota(jnp.int32, (8, T), 1)
    sub = lax.broadcasted_iota(jnp.int32, (8, T), 0)
    own = [sub == j for j in range(8)]
    out = []

    def splat(x, c):
        return jnp.broadcast_to(x[:, c:c + 1], (8, T))

    ahead = [splat(rows[0], c) for c in range(8)]
    for k in range(16):
        last = k == 15
        inside = (lane >= 8 * k) & (lane < 8 * k + 8)
        b = ahead
        later = [] if last else [splat(rows[k], 8 * k + 8 + c) for c in range(8)]
        cols = [[splat(r, 8 * k + j) for j in range(8)] for r in rows[k + 1:k + 1 + ND]]
        fresh = [] if last else [splat(rows[k + 1], 8 * k + 8 + c) for c in range(8)]
        panel = jnp.where(inside, jnp.where(lane - 8 * k == sub, 1.0, 0.0), rows[k])
        done = jnp.zeros((8, T), jnp.float32)
        for j in range(8):
            p = row_of(b[j], j)
            r = 1.0 / p
            f = b[j]

            def clear(x):
                n = row_of(x, j) * r
                return jnp.where(own[j], n, x - f * n)

            done = jnp.where(own[j], row_of(panel, j) * lax.rsqrt(p), done)
            for l in range(j + 1, 8):
                b[l] = clear(b[l])
            later = [clear(x) for x in later]
            panel = clear(panel)
        out.append(jnp.where(lane < 8 * k + 8, done, 0.0))
        if last:
            break
        ahead = []
        for c in range(8):
            terms = [cols[0][j] * row_of(later[c], j) for j in range(8)]
            while len(terms) > 1:
                terms = [terms[i] + terms[i + 1] for i in range(0, len(terms), 2)]
            ahead.append(fresh[c] - terms[0])
        spread = [row_of(panel, j) for j in range(8)]
        near = min(k + 1 + ND, 16)
        if near < 16:
            wide = [jnp.zeros((8, T), jnp.float32)] * 16
            wide[k] = panel
            away = dot(jnp.concatenate(rows[near:], axis=0), jnp.concatenate(wide, axis=0))
        for g in range(k + 1, 16):
            acc = jnp.where(inside, 0.0, rows[g])
            if g < near:
                for j in range(8):
                    acc = acc - cols[g - k - 1][j] * spread[j]
            else:
                acc = acc - away[8 * (g - near):8 * (g - near) + 8]
            rows[g] = acc
    return out

def solve_kernel(c_ref, x_ref, d_hbm, r_hbm, high_hbm, image_hbm, out_d_ref, out_r_ref,
                 a_ref, l_ref, v_ref, z_ref, d_ref, r_ref, high_ref, image_ref, sem):
    fetches = [pltpu.make_async_copy(a, b, sem.at[i]) for i, (a, b) in enumerate((
        (d_hbm, d_ref), (r_hbm, r_ref), (high_hbm, high_ref), (image_hbm, image_ref)))]
    for fetch in fetches:
        fetch.start()
    n = c_ref.shape[0]
    nb = n // T
    wide = n + T
    for i in range(nb):
        for j in range(i, nb):
            a_ref[i * T:(i + 1) * T, j * T:(j + 1) * T] = 0.5 * (
                c_ref[i * T:(i + 1) * T, j * T:(j + 1) * T] + c_ref[j * T:(j + 1) * T, i * T:(i + 1) * T].T)
    start = pl.multiple_of(lax.axis_index("cls") * T, T)
    for i in range(nb):
        here = slice(i * T, (i + 1) * T)
        a_ref[here, n:] = (x_ref[:, here] + 0.5 * c_ref[pl.ds(start, T), here]).T - 0.5 * c_ref[here, pl.ds(start, T)]
    def update(k, i):
        here, there = slice(k * T, (k + 1) * T), slice(i * T, (i + 1) * T)
        a_ref[there, i * T:] -= dot(v_ref[here, there], v_ref[here, i * T:], ((0,), (0,)))

    for k in range(nb):
        here = slice(k * T, (k + 1) * T)
        rows = factor([a_ref[k * T + 8 * g:k * T + 8 * g + 8, here] for g in range(16)])
        for i in range(k + 1, nb):
            if k:
                update(k - 1, i)
        for g in range(16):
            l_ref[k * T + 8 * g:k * T + 8 * g + 8, :] = rows[g]
        v_ref[here, (k + 1) * T:] = dot(l_ref[here, :], a_ref[here, (k + 1) * T:])
        if k + 1 < nb:
            update(k, k + 1)
    y = v_ref[:, n:]
    for j in range(nb - 1, -1, -1):
        here = slice(j * T, (j + 1) * T)
        known = dot(l_ref[here, :], y[here], ((0,), (0,)))
        z_ref[here, :] = known
        if j:
            y = y[:j * T] - dot(v_ref[:j * T, here], known)
    for fetch in fetches:
        fetch.wait()
    top = z_ref[...].astype(jnp.bfloat16)
    both = jnp.concatenate([top, (z_ref[...] - top.astype(jnp.float32)).astype(jnp.bfloat16)], axis=1)

    def products(t, _):
        at = pl.ds(pl.multiple_of(t * 2 * T, 2 * T), 2 * T)

        def row(ref):
            return jnp.concatenate([ref[m, at, :] for m in range(ref.shape[0])], axis=1)

        def times(a, b):
            return jnp.dot(a, b, preferred_element_type=jnp.float32)

        out_d_ref[at, :] = d_ref[at, :] + times(row(high_ref), top)
        pair = times(row(image_ref.at[0]), both)
        out_r_ref[at, :] = r_ref[at, :] - (pair[:, :T] + (pair[:, T:] + times(row(image_ref.at[1]), top)))
        return 0

    lax.fori_loop(0, d_ref.shape[0] // (2 * T), products, 0)


def solve(c, x, direction, misfit, high, image):
    n = c.shape[0]
    rows = direction.shape[0]
    f32 = jnp.float32
    vmem, hbm = pl.BlockSpec(memory_space=pltpu.VMEM), pl.BlockSpec(memory_space=pl.ANY)
    return pl.pallas_call(
        solve_kernel,
        out_shape=[jax.ShapeDtypeStruct((rows, T), f32)] * 2,
        in_specs=[vmem] * 2 + [hbm] * 4,
        out_specs=[vmem] * 2,
        scratch_shapes=[pltpu.VMEM((n, n + T), f32), pltpu.VMEM((n, T), f32), pltpu.VMEM((n, n + T), f32),
                        pltpu.VMEM((n, T), f32), pltpu.VMEM((rows, T), f32), pltpu.VMEM((rows, T), f32),
                        pltpu.VMEM(high.shape, high.dtype), pltpu.VMEM(image.shape, image.dtype),
                        pltpu.SemaphoreType.DMA((4,))],
        compiler_params=pltpu.CompilerParams(vmem_limit_bytes=63 << 20),
    )(c, x, direction, misfit, high, image)


def body(seed_scores, tile_vals, tile_cols, tile_count, tile_scale):
    slots, weights = by_offset(tile_cols, tile_count, tile_scale)
    tiles = tile_vals.reshape(-1, T, T)
    direction, misfit, parts, high, ct, xt = find_direction(slots, weights, seed_scores, tiles)
    full, xs, image = sum_and_share(ct, xt, parts)
    return tuple(solve(full, xs, direction, misfit, high, image))


def solution(mesh):
    return jax.shard_map(
        body,
        mesh=mesh,
        in_specs=(
            P("node", "cls"),
            P("node", None, None, None),
            P("node", None),
            P("node"),
            P("node", None),
        ),
        out_specs=(P("node", "cls"), P("node", "cls")),
        check_vma=False,
    )
```

```python
import functools
import jax
import jax.numpy as jnp
from jax import lax
from jax.experimental import pallas as pl
from jax.experimental.pallas import tpu as pltpu
from jax.sharding import PartitionSpec as P

SHRINK = 0.9
HI = lax.Precision.HIGHEST
MESH = pl.DeviceIdType.MESH
T = 128
GUESS = (-2.9, 2.34)


def remote(src, dst, send, recv, to):
    return pltpu.make_async_remote_copy(
        src_ref=src, dst_ref=dst, send_sem=send, recv_sem=recv, device_id=to, device_id_type=MESH)


def greet(peers):
    barrier = pltpu.get_barrier_semaphore()
    for peer in peers:
        pl.semaphore_signal(barrier, inc=1, device_id=peer, device_id_type=MESH)
    pl.semaphore_wait(barrier, len(peers))


def direction_kernel(slot_ref, weight_ref, seed_ref, tiles_hbm,
                     d_ref, r_ref, parts_ref, spread_hbm, ct_ref, xt_ref,
                     tiles_ref, ext_ref, acc_ref, z_ref, all_ref, flat_ref, sum_ref, tiles_sem, out_sem,
                     halo_send, halo_recv, ring_send, ring_recv, pair_send, pair_recv):
    fetch = pltpu.make_async_copy(tiles_hbm, tiles_ref, tiles_sem)
    fetch.start()
    blocks = acc_ref.shape[0] // T
    reach = 8
    rows = blocks * T
    half = rows // 2
    edge = reach * T
    node, cls = lax.axis_index("node"), lax.axis_index("cls")
    nodes = lax.axis_size("node")
    chips = lax.axis_size("cls") // 2
    chip, core = cls // 2, cls % 2
    right_node, left_node = {"node": (node + 1) % nodes}, {"node": (node + nodes - 1) % nodes}
    right_chip, left_chip, far_chip = (chip + 1) % chips, (chip + chips - 1) % chips, (chip + 2) % chips
    right, left, twin = {"cls": right_chip * 2 + core}, {"cls": left_chip * 2 + core}, {"cls": chip * 2 + 1 - core}
    greet([right_node, left_node, right, left, twin])

    def halo_copies(s):
        ext = ext_ref.at[s]
        return (
            remote(ext.at[pl.ds(rows, edge)], ext.at[pl.ds(0, edge)],
                   halo_send.at[s, 0], halo_recv.at[s, 0], right_node),
            remote(ext.at[pl.ds(edge, edge)], ext.at[pl.ds(edge + rows, edge)],
                   halo_send.at[s, 1], halo_recv.at[s, 1], left_node),
        )

    def product(s, tile, source):
        return jnp.dot(tiles_ref[tile], ext_ref[s, pl.ds(pl.multiple_of(source * T, T), T), :],
                       preferred_element_type=jnp.float32)

    def spread(s, z):
        ext_ref[s, edge:edge + rows, :] = z.astype(jnp.bfloat16)
        copies = halo_copies(s)
        for copy in copies:
            copy.start()
        return copies

    def local_part(s):
        def one(i, _):
            total = jnp.zeros((T, T), jnp.float32)
            for j in range(blocks):
                o = j + reach - i
                fits = (o >= 0) & (o <= 2 * reach)
                at = i * (2 * reach + 1) + jnp.clip(o, 0, 2 * reach)
                w = jnp.where(fits, weight_ref[at], 0.0)
                total += w * product(s, slot_ref[at], j + reach)
            acc_ref[pl.ds(pl.multiple_of(i * T, T), T), :] = total
            return 0
        lax.fori_loop(0, blocks, one, 0)

    def edge_part(s):
        def one(t, _):
            low = jnp.zeros((T, T), jnp.float32)
            high = jnp.zeros((T, T), jnp.float32)
            for m in range(reach + 1):
                lower = m < reach - t
                i = jnp.where(lower, t, t + blocks - reach)
                j = t + m + jnp.where(lower, 0, blocks)
                at = i * (2 * reach + 1) + j - i
                w = weight_ref[at]
                p = product(s, slot_ref[at], j)
                low += jnp.where(lower, w, 0.0) * p
                high += jnp.where(lower, 0.0, w) * p
            acc_ref[pl.ds(pl.multiple_of(t * T, T), T), :] += low
            acc_ref[pl.ds(pl.multiple_of((t + blocks - reach) * T, T), T), :] += high
            return 0
        lax.fori_loop(0, reach, one, 0)

    def operate(s, copies):
        local_part(s)
        for copy in copies:
            copy.wait_recv()
        edge_part(s)

    def ring_copy(q, n, owner, part, to):
        ref = all_ref.at[q, owner, pl.ds(part * half, half)]
        return remote(ref, ref, ring_send.at[q, n], ring_recv.at[q, n], to)

    def twin_copy(q, n, owner):
        ref = all_ref.at[q, owner]
        return remote(ref, ref, pair_send.at[q, n], pair_recv.at[q, n], twin)

    pending = []

    def go(copies):
        for copy in copies:
            copy.start()
        pending.extend(copies)
        return copies

    def ring_first(q, value):
        all_ref[q, cls] = value.astype(jnp.bfloat16)
        return go([ring_copy(q, 0, cls, 0, right), ring_copy(q, 1, cls, 1, left),
                   ring_copy(q, 2, cls, 1, right), ring_copy(q, 3, cls, 0, left)]), go([twin_copy(q, 0, cls)])

    def ring_second(q, sent):
        sent[0].wait_recv()
        a = go([ring_copy(q, 4, left_chip * 2 + core, 0, right)])
        sent[1].wait_recv()
        b = go([ring_copy(q, 5, right_chip * 2 + core, 1, left)])
        sent[2].wait_recv()
        c = go([twin_copy(q, 1, left_chip * 2 + core)])
        sent[3].wait_recv()
        d = go([twin_copy(q, 2, right_chip * 2 + core)])
        return a + b, c, d

    def ring_last(q, sent):
        for copy in sent:
            copy.wait_recv()
        return go([twin_copy(q, 3, far_chip * 2 + core)])

    def grams(q, which):
        both = jnp.concatenate([all_ref[q, which * 2], all_ref[q, which * 2 + 1]], axis=1)
        at = pl.ds(pl.multiple_of(which * 2 * T, 2 * T), 2 * T)
        out = jnp.dot(flat_ref[...], both, preferred_element_type=jnp.float32)
        image_part, r_part = out[0:T] + out[2 * T:3 * T], out[T:2 * T] + out[3 * T:]
        if q == 0:
            ct_ref[:, at] = image_part
            xt_ref[:, at] = r_part
        else:
            ct_ref[:, at] += image_part
            xt_ref[:, at] += r_part

    def keep(m):
        def one(t, _):
            at = pl.ds(pl.multiple_of(t * T, T), T)
            for n in range(2):
                total = all_ref[0, 2 * m + n, at, :].astype(jnp.float32) + all_ref[1, 2 * m + n, at, :].astype(jnp.float32)
                total = total + all_ref[2, 2 * m + n, at, :].astype(jnp.float32)
                sum_ref[2 * m + n, at, :] = total.astype(jnp.bfloat16)
            return 0
        lax.fori_loop(0, blocks, one, 0)
        at = pl.ds(2 * m, 2)
        return pltpu.make_async_copy(sum_ref.at[at], spread_hbm.at[at], out_sem.at[m])

    factor = SHRINK
    z_ref[...] = seed_ref[...]
    d_ref[...] = seed_ref[...]
    firsts, owns, seconds = [], [], []
    for s in range(2):
        copies = spread(s, z_ref[...])
        pending.extend(copies)
        if s:
            seconds.append(ring_second(0, firsts[0]))
        first, own = ring_first(s, GUESS[s] * z_ref[...])
        firsts.append(first)
        owns.append(own)
        if s == 0:
            fetch.wait()
        operate(s, copies)
        factor_next = 1.0 / (2.0 / SHRINK - factor)
        misfit = seed_ref[...] - (z_ref[...] - SHRINK * acc_ref[...])
        update = factor_next * factor * d_ref[...] + (2.0 * factor_next / SHRINK) * misfit
        d_ref[...] = update
        z_ref[...] = z_ref[...] + update
        factor = factor_next
    z = z_ref[...]
    d_ref[...] = z
    copies = spread(2, z)
    pending.extend(copies)
    seconds.append(ring_second(1, firsts[1]))
    first, own = ring_first(2, z - all_ref[0, cls].astype(jnp.float32) - all_ref[1, cls].astype(jnp.float32))
    lasts = [ring_last(0, seconds[0][0])]
    operate(2, copies)
    second = ring_second(2, first)
    image = z_ref[...] - SHRINK * acc_ref[...]
    r_ref[...] = seed_ref[...] - image
    coarse = image.astype(jnp.bfloat16)
    parts_ref[...] = coarse
    lasts.append(ring_last(1, seconds[1][0]))

    image_t = image.T
    r_t = r_ref[...].T
    for n, value in enumerate((image_t, r_t)):
        top = value.astype(jnp.bfloat16)
        flat_ref[n * T:(n + 1) * T, :] = top
        flat_ref[(2 + n) * T:(3 + n) * T, :] = (value - top.astype(jnp.float32)).astype(jnp.bfloat16)

    for q in range(2):
        for copy in owns[q] + list(seconds[q][1]) + list(seconds[q][2]) + lasts[q]:
            copy.wait_recv()
        for m in range(chips):
            grams(q, m)
    kept = []

    def third(m):
        grams(2, m)
        kept.append(keep(m))
        kept[-1].start()

    own[0].wait_recv()
    third(chip)
    last = ring_last(2, second[0])
    second[1][0].wait_recv()
    third(left_chip)
    second[2][0].wait_recv()
    third(right_chip)
    last[0].wait_recv()
    third(far_chip)
    for copy in pending:
        copy.wait_send()
    for copy in kept:
        copy.wait()


def find_direction(slots, weights, seed, tiles):
    rows, width = seed.shape
    every = lax.axis_size("cls")
    f32 = jnp.float32
    vmem = pl.BlockSpec(memory_space=pltpu.VMEM)
    smem = pl.BlockSpec(memory_space=pltpu.SMEM)
    hbm = pl.BlockSpec(memory_space=pl.ANY)
    sems = pltpu.SemaphoreType.DMA
    return pl.pallas_call(
        direction_kernel,
        out_shape=[
            jax.ShapeDtypeStruct((rows, width), f32),
            jax.ShapeDtypeStruct((rows, width), f32),
            jax.ShapeDtypeStruct((rows, width), jnp.bfloat16),
            jax.ShapeDtypeStruct((every, rows, width), jnp.bfloat16),
            jax.ShapeDtypeStruct((width, every * width), f32),
            jax.ShapeDtypeStruct((width, every * width), f32),
        ],
        in_specs=[smem, smem, vmem, hbm],
        out_specs=[vmem] * 3 + [hbm] + [vmem] * 2,
        scratch_shapes=[
            pltpu.VMEM(tiles.shape, tiles.dtype),
            pltpu.VMEM((3, rows + 16 * T, width), jnp.bfloat16),
            pltpu.VMEM((rows, width), f32),
            pltpu.VMEM((rows, width), f32),
            pltpu.VMEM((3, every, rows, width), jnp.bfloat16),
            pltpu.VMEM((4 * T, rows), jnp.bfloat16),
            pltpu.VMEM((every, rows, width), jnp.bfloat16),
            sems(()), sems((4,)),
            sems((3, 2)), sems((3, 2)), sems((3, 6)), sems((3, 6)), sems((3, 4)), sems((3, 4)),
        ],
        compiler_params=pltpu.CompilerParams(collective_id=0, has_side_effects=True, vmem_limit_bytes=48 << 20),
    )(slots, weights, seed, tiles)


def by_offset(tile_cols, tile_count, tile_scale):
    local_blocks, slot_total = tile_cols.shape
    reach = (slot_total - 1) // 2
    total = local_blocks * lax.axis_size("node")
    row = jnp.arange(local_blocks)[:, None]
    where = jnp.mod(tile_cols - (lax.axis_index("node") * local_blocks + row) + reach, total)
    slot = jnp.arange(slot_total)[None, :]
    weights = jnp.where(slot < tile_count[:, None], tile_scale, 0.0)
    hit = where[:, :, None] == jnp.arange(slot_total)[None, None, :]
    slots = jnp.sum(jnp.where(hit, (row * slot_total + slot)[:, :, None], 0), axis=1)
    return slots.reshape(-1), jnp.sum(jnp.where(hit, weights[:, :, None], 0.0), axis=1).reshape(-1)


def sum_kernel(ct_ref, xt_ref, parts_ref, full_ref, xs_ref, image_ref,
               first_ref, part_ref, second_ref,
               send1, recv1, send2, recv2, send_a, recv_a, send_b, recv_b, send_c, recv_c,
               send_t, recv_t, send_xb, recv_xb, send_xc, recv_xc, ring_send, ring_recv, pair_send, pair_recv, place_sem):
    side = 4
    node, cls = lax.axis_index("node"), lax.axis_index("cls")
    chip, core = cls // 2, cls % 2
    y, z = node // side, node % side
    f = jnp.where(core == 0, z, y)
    s = jnp.where(core == 0, y, z)
    rows = parts_ref.shape[0]
    half = rows // 2

    def at(f_, s_):
        return {"node": jnp.where(core == 0, s_ * side + f_, f_ * side + s_)}

    def turn(v, m):
        return (v + m) % side

    along_f = [at(turn(f, m), s) for m in range(1, side)]
    along_s = [at(f, turn(s, m)) for m in range(1, side)]
    along_x = [{"cls": turn(chip, m) * 2 + core} for m in range(1, side)]
    twin = {"cls": chip * 2 + 1 - core}
    greet(along_f + along_s + along_x + [twin])

    pending = []

    def go(copies):
        for copy in copies:
            copy.start()
        pending.extend(copies)
        return copies

    grams = (ct_ref, xt_ref)

    def stage1(q):
        return go([remote(grams[q].at[:, turn(f, m)], first_ref.at[q, m - 1],
                          send1.at[q, m - 1], recv1.at[q, m - 1], along_f[m - 1])
                   for m in range(1, side)])

    def stage2(q, before):
        for copy in before:
            copy.wait_recv()
        for k in range(side):
            part_ref[q, k] = (grams[q][k, f] + first_ref[q, 0, k]) + (first_ref[q, 1, k] + first_ref[q, 2, k])
        return go([remote(part_ref.at[q, turn(s, m)], second_ref.at[q, m - 1],
                          send2.at[q, m - 1], recv2.at[q, m - 1], along_s[m - 1])
                   for m in range(1, side)])

    def finish(q, before):
        for copy in before:
            copy.wait_recv()
        return (part_ref[q, s] + second_ref[q, 0]) + (second_ref[q, 1] + second_ref[q, 2])

    before, after, across = turn(chip, 3), turn(chip, 1), turn(chip, 2)
    to_right, to_left = along_x[0], along_x[2]

    def ring_copy(q, n, owner, part, to):
        ref = image_ref.at[q, owner, pl.ds(part * half, half)]
        return remote(ref, ref, ring_send.at[q, n], ring_recv.at[q, n], to)

    def pair_copy(q, n, owner):
        ref = image_ref.at[q, owner]
        return remote(ref, ref, pair_send.at[q, n], pair_recv.at[q, n], twin)

    def image_first(q):
        return go([ring_copy(q, 0, cls, 0, to_right), ring_copy(q, 1, cls, 1, to_left),
                   ring_copy(q, 2, cls, 1, to_right), ring_copy(q, 3, cls, 0, to_left)])

    def image_second(q, sent):
        sent[0].wait_recv()
        a = go([ring_copy(q, 4, before * 2 + core, 0, to_right)])
        sent[1].wait_recv()
        b = go([ring_copy(q, 5, after * 2 + core, 1, to_left)])
        sent[2].wait_recv()
        c = go([pair_copy(q, 1, before * 2 + core)])
        sent[3].wait_recv()
        d = go([pair_copy(q, 2, after * 2 + core)])
        return a + b, c + d

    def image_last(q, sent):
        for copy in sent:
            copy.wait_recv()
        return go([pair_copy(q, 3, across * 2 + core)])

    c1 = stage1(0)
    place = [pltpu.make_async_copy(parts_ref, image_ref.at[0, cls], place_sem.at[0])]
    for copy in place:
        copy.start()
    for copy in place:
        copy.wait()
    top1 = image_first(0)
    c2 = stage2(0, c1)
    x1 = stage1(1)
    full_ref[chip, core, s, f] = finish(0, c2)
    mine = full_ref.at[chip, core, s, f]
    stage_a = go([remote(mine, mine, send_a.at[m], recv_a.at[m], along_x[m]) for m in range(side - 1)])
    x2 = stage2(1, x1)
    for copy in stage_a:
        copy.wait_recv()
    line = full_ref.at[:, core, s, f]
    stage_b = go([remote(line, line, send_b.at[m], recv_b.at[m], along_f[m]) for m in range(side - 1)])
    shared_image = go([pair_copy(0, 0, cls)])
    xs_ref[s, f] = finish(1, x2)
    mine_x = xs_ref.at[s, f]
    stage_xb = go([remote(mine_x, mine_x, send_xb.at[m], recv_xb.at[m], along_f[m]) for m in range(side - 1)])
    top2, more = image_second(0, top1)
    shared_image += more
    for copy in stage_b:
        copy.wait_recv()

    def slab(owner, h):
        return full_ref.at[pl.ds(2 * h, 2), core, owner]

    def ring(n, owner, h, to):
        return remote(slab(owner, h), slab(owner, h), send_c.at[n], recv_c.at[n], to)

    def share(n, owner, h):
        return remote(slab(owner, h), slab(owner, h), send_t.at[n], recv_t.at[n], twin)

    up, down = along_s[0], along_s[2]
    below, above, far = turn(s, 3), turn(s, 1), turn(s, 2)
    r0, r1, r2, r3 = go([ring(0, s, 0, up), ring(1, s, 1, down), ring(2, s, 1, up), ring(3, s, 0, down)])
    shared = go([share(0, s, 0), share(1, s, 1)])
    for copy in stage_xb:
        copy.wait_recv()
    line_x = xs_ref.at[s]
    stage_xc = go([remote(line_x, line_x, send_xc.at[m], recv_xc.at[m], along_s[m]) for m in range(side - 1)])
    r0.wait_recv()
    fwd0, = go([ring(4, below, 0, up)])
    r1.wait_recv()
    fwd1, = go([ring(5, above, 1, down)])
    shared += go([share(2, below, 0), share(3, above, 1)])
    shared_image += image_last(0, top2)
    r2.wait_recv()
    shared += go([share(4, below, 1)])
    r3.wait_recv()
    shared += go([share(5, above, 0)])
    fwd0.wait_recv()
    shared += go([share(6, far, 0)])
    fwd1.wait_recv()
    shared += go([share(7, far, 1)])
    for copy in stage_xc + shared + shared_image:
        copy.wait_recv()
    for copy in pending:
        copy.wait_send()


def sum_and_share(ct, xt, parts):
    width, classes = ct.shape
    f32 = jnp.float32
    vmem = pl.BlockSpec(memory_space=pltpu.VMEM)
    sems = pltpu.SemaphoreType.DMA
    cut = (4, 4, width // 16, classes)
    hbm = pl.BlockSpec(memory_space=pl.ANY)
    rows = parts.shape[0]
    full, xs, image = pl.pallas_call(
        sum_kernel,
        out_shape=[jax.ShapeDtypeStruct((4, 2) + cut, f32), jax.ShapeDtypeStruct(cut, f32),
                   jax.ShapeDtypeStruct((1, classes // width, rows, width), parts.dtype)],
        in_specs=[vmem, vmem, hbm],
        out_specs=[vmem, vmem, hbm],
        scratch_shapes=[
            pltpu.VMEM((2, 3, 4, width // 16, classes), f32),
            pltpu.VMEM((2, 4, width // 16, classes), f32),
            pltpu.VMEM((2, 3, width // 16, classes), f32),
            sems((2, 3)), sems((2, 3)), sems((2, 3)), sems((2, 3)),
            sems((3,)), sems((3,)), sems((3,)), sems((3,)), sems((6,)), sems((6,)),
            sems((8,)), sems((8,)), sems((3,)), sems((3,)), sems((3,)), sems((3,)),
            sems((1, 6)), sems((1, 6)), sems((1, 4)), sems((1, 4)), sems((1,)),
        ],
        compiler_params=pltpu.CompilerParams(collective_id=1, has_side_effects=True, vmem_limit_bytes=32 << 20),
    )(ct.reshape(cut), xt.reshape(cut), parts)
    return full.reshape(classes, classes), xs.reshape(width, classes), image


ND = 2

def dot(a, b, dims=((1,), (0,))):
    return lax.dot_general(a, b, (dims, ((), ())), precision=HI, preferred_element_type=jnp.float32)

def row_of(x, j):
    return jnp.broadcast_to(x[j:j + 1, :], (8, T))

def factor(rows):
    lane = lax.broadcasted_iota(jnp.int32, (8, T), 1)
    sub = lax.broadcasted_iota(jnp.int32, (8, T), 0)
    own = [sub == j for j in range(8)]
    out = []

    def splat(x, c):
        return jnp.broadcast_to(x[:, c:c + 1], (8, T))

    ahead = [splat(rows[0], c) for c in range(8)]
    for k in range(16):
        last = k == 15
        inside = (lane >= 8 * k) & (lane < 8 * k + 8)
        b = ahead
        later = [] if last else [splat(rows[k], 8 * k + 8 + c) for c in range(8)]
        cols = [[splat(r, 8 * k + j) for j in range(8)] for r in rows[k + 1:k + 1 + ND]]
        fresh = [] if last else [splat(rows[k + 1], 8 * k + 8 + c) for c in range(8)]
        panel = jnp.where(inside, jnp.where(lane - 8 * k == sub, 1.0, 0.0), rows[k])
        done = jnp.zeros((8, T), jnp.float32)
        for j in range(8):
            p = row_of(b[j], j)
            r = 1.0 / p
            f = b[j]

            def clear(x):
                n = row_of(x, j) * r
                return jnp.where(own[j], n, x - f * n)

            done = jnp.where(own[j], row_of(panel, j) * lax.rsqrt(p), done)
            for l in range(j + 1, 8):
                b[l] = clear(b[l])
            later = [clear(x) for x in later]
            panel = clear(panel)
        out.append(jnp.where(lane < 8 * k + 8, done, 0.0))
        if last:
            break
        ahead = []
        for c in range(8):
            terms = [cols[0][j] * row_of(later[c], j) for j in range(8)]
            while len(terms) > 1:
                terms = [terms[i] + terms[i + 1] for i in range(0, len(terms), 2)]
            ahead.append(fresh[c] - terms[0])
        spread = [row_of(panel, j) for j in range(8)]
        near = min(k + 1 + ND, 16)
        if near < 16:
            wide = [jnp.zeros((8, T), jnp.float32)] * 16
            wide[k] = panel
            away = dot(jnp.concatenate(rows[near:], axis=0), jnp.concatenate(wide, axis=0))
        for g in range(k + 1, 16):
            acc = jnp.where(inside, 0.0, rows[g])
            if g < near:
                for j in range(8):
                    acc = acc - cols[g - k - 1][j] * spread[j]
            else:
                acc = acc - away[8 * (g - near):8 * (g - near) + 8]
            rows[g] = acc
    return out

def solve_kernel(c_ref, x_ref, d_hbm, r_hbm, high_hbm, image_hbm, out_d_ref, out_r_ref,
                 a_ref, l_ref, v_ref, z_ref, d_ref, r_ref, high_ref, image_ref, sem):
    fetches = [pltpu.make_async_copy(a, b, sem.at[i]) for i, (a, b) in enumerate((
        (d_hbm, d_ref), (r_hbm, r_ref), (high_hbm, high_ref), (image_hbm, image_ref)))]
    for fetch in fetches:
        fetch.start()
    n = c_ref.shape[0]
    nb = n // T
    wide = n + T
    for i in range(nb):
        for j in range(i, nb):
            a_ref[i * T:(i + 1) * T, j * T:(j + 1) * T] = 0.5 * (
                c_ref[i * T:(i + 1) * T, j * T:(j + 1) * T] + c_ref[j * T:(j + 1) * T, i * T:(i + 1) * T].T)
    start = pl.multiple_of(lax.axis_index("cls") * T, T)
    for i in range(nb):
        here = slice(i * T, (i + 1) * T)
        a_ref[here, n:] = (x_ref[:, here] + 0.5 * c_ref[pl.ds(start, T), here]).T - 0.5 * c_ref[here, pl.ds(start, T)]
    def update(k, i):
        here, there = slice(k * T, (k + 1) * T), slice(i * T, (i + 1) * T)
        a_ref[there, i * T:] -= dot(v_ref[here, there], v_ref[here, i * T:], ((0,), (0,)))

    for k in range(nb):
        here = slice(k * T, (k + 1) * T)
        rows = factor([a_ref[k * T + 8 * g:k * T + 8 * g + 8, here] for g in range(16)])
        for i in range(k + 1, nb):
            if k:
                update(k - 1, i)
        for g in range(16):
            l_ref[k * T + 8 * g:k * T + 8 * g + 8, :] = rows[g]
        v_ref[here, (k + 1) * T:] = dot(l_ref[here, :], a_ref[here, (k + 1) * T:])
        if k + 1 < nb:
            update(k, k + 1)
    y = v_ref[:, n:]
    for j in range(nb - 1, -1, -1):
        here = slice(j * T, (j + 1) * T)
        known = dot(l_ref[here, :], y[here], ((0,), (0,)))
        z_ref[here, :] = known
        if j:
            y = y[:j * T] - dot(v_ref[:j * T, here], known)
    for fetch in fetches:
        fetch.wait()
    top = z_ref[...].astype(jnp.bfloat16)
    both = jnp.concatenate([top, (z_ref[...] - top.astype(jnp.float32)).astype(jnp.bfloat16)], axis=1)

    def products(t, _):
        at = pl.ds(pl.multiple_of(t * 6 * T, 6 * T), 6 * T)

        def row(ref):
            return jnp.concatenate([ref[m, at, :] for m in range(ref.shape[0])], axis=1)

        def times(a, b):
            return jnp.dot(a, b, preferred_element_type=jnp.float32)

        out_d_ref[at, :] = d_ref[at, :] + times(row(high_ref), top)
        pair = times(row(image_ref.at[0]), both)
        out_r_ref[at, :] = r_ref[at, :] - (pair[:, :T] + pair[:, T:])
        return 0

    lax.fori_loop(0, d_ref.shape[0] // (6 * T), products, 0)


def solve(c, x, direction, misfit, high, image):
    n = c.shape[0]
    rows = direction.shape[0]
    f32 = jnp.float32
    vmem, hbm = pl.BlockSpec(memory_space=pltpu.VMEM), pl.BlockSpec(memory_space=pl.ANY)
    return pl.pallas_call(
        solve_kernel,
        out_shape=[jax.ShapeDtypeStruct((rows, T), f32)] * 2,
        in_specs=[vmem] * 2 + [hbm] * 4,
        out_specs=[vmem] * 2,
        scratch_shapes=[pltpu.VMEM((n, n + T), f32), pltpu.VMEM((n, T), f32), pltpu.VMEM((n, n + T), f32),
                        pltpu.VMEM((n, T), f32), pltpu.VMEM((rows, T), f32), pltpu.VMEM((rows, T), f32),
                        pltpu.VMEM(high.shape, high.dtype), pltpu.VMEM(image.shape, image.dtype),
                        pltpu.SemaphoreType.DMA((4,))],
        compiler_params=pltpu.CompilerParams(vmem_limit_bytes=63 << 20),
    )(c, x, direction, misfit, high, image)


def body(seed_scores, tile_vals, tile_cols, tile_count, tile_scale):
    slots, weights = by_offset(tile_cols, tile_count, tile_scale)
    tiles = tile_vals.reshape(-1, T, T)
    direction, misfit, parts, high, ct, xt = find_direction(slots, weights, seed_scores, tiles)
    full, xs, image = sum_and_share(ct, xt, parts)
    return tuple(solve(full, xs, direction, misfit, high, image))


def solution(mesh):
    return jax.shard_map(
        body,
        mesh=mesh,
        in_specs=(
            P("node", "cls"),
            P("node", None, None, None),
            P("node", None),
            P("node"),
            P("node", None),
        ),
        out_specs=(P("node", "cls"), P("node", "cls")),
        check_vma=False,
    )
```
